128 devices in a mesh: genome: 16 (over z, x), trow: 2 (over core), tcol: 4 (over y).
Axes of the slice: x: 4, y: 4, z: 4, core: 2. Of those that a mesh axis runs over, the one named last changes fastest.
Arguments:
- ldscore: float32 [16384], P('genome'), may hold values from 1 to 100
- zscores: bfloat16 [16384, 4096], P('genome', ('trow', 'tcol')), may hold values from -30 to 30
Outputs:
- rg: float32 [2, 2048, 2, 2048], P('trow', 'genome', None, 'tcol')
- rg_se: float32 [2, 2048, 2, 2048], P('trow', 'genome', None, 'tcol')
The draws below stay inside these ranges and needn't reach their ends.
All inputs are finite; a program needn't handle non-finite values.
Results may differ from the reference program's by a relative error of at most 0.038.
Values may be sent and summed in bfloat16 or wider, within the bound.
A program may use at most 192 MiB of HBM per device.

```python
import math
import jax
import jax.numpy as jnp
from jax import lax

TRAITS = 4096
S_DEV = 1024
SNPS = 16384
N_GENOME = 16
N_TROW = 2


def ld_table(key):
    block_count = SNPS // S_DEV
    centre = jax.random.uniform(jax.random.fold_in(key, 21), (block_count,), jnp.float32, math.log(1.2), math.log(60.0))
    within = jax.random.uniform(jax.random.fold_in(key, 11), (block_count, S_DEV), jnp.float32, -0.7, 0.7)
    raw = (centre[:, None] + within).reshape(SNPS)
    return jnp.clip(jnp.exp(raw), 1.0, 100.0)


def draw_ldscore(key, part):
    return ld_table(key)


def draw_zscores(key, part):
    ld_vals = ld_table(key)
    top_herit = 0.05
    herit = jnp.exp(jax.random.uniform(jax.random.fold_in(key, 12), (TRAITS,), jnp.float32, math.log(0.0008), math.log(top_herit)))
    group = jax.random.randint(jax.random.fold_in(key, 13), (TRAITS,), 0, 8)
    noise_group = jax.random.randint(jax.random.fold_in(key, 18), (TRAITS,), 0, 8)
    share = jax.random.uniform(jax.random.fold_in(key, 14), (TRAITS,), jnp.float32, 0.3, 0.95)
    common = jax.random.normal(jax.random.fold_in(key, 15), (SNPS, 8), jnp.float32)
    private = jax.random.normal(jax.random.fold_in(key, 16), (SNPS, TRAITS), jnp.float32)
    own_noise = jax.random.normal(jax.random.fold_in(key, 17), (SNPS, TRAITS), jnp.float32)
    shared_noise = jax.random.normal(jax.random.fold_in(key, 19), (SNPS, 8), jnp.float32)
    picked = jnp.take(common, group, axis=1)
    genetic = share[None, :] * picked + jnp.sqrt(1.0 - share * share)[None, :] * private
    noise = math.sqrt(0.85) * own_noise + math.sqrt(0.15) * jnp.take(shared_noise, noise_group, axis=1)
    zvalue = noise + jnp.sqrt(herit[None, :] * ld_vals[:, None]) * genetic
    return jnp.clip(zvalue, -30.0, 30.0).astype(jnp.bfloat16)


def setup_inputs(seed: int = 0) -> dict:
    seeds = jax.random.split(jax.random.key(seed), 3)
    ldscore = draw_ldscore(jax.random.fold_in(seeds[2], 71), 0)
    zscores = draw_zscores(jax.random.fold_in(seeds[2], 71), 0)
    return {"ldscore": ldscore, "zscores": zscores}


floor_value = 0.002

def slope_fit(inv_sum, ld_sum, y_sum, l_sum, count):
    return (inv_sum * l_sum - count * y_sum) / (inv_sum * ld_sum - count * count)

def weights_for(herit_pos, ld_column):
    return (1.0 / (1.0 + herit_pos[None, :] * ld_column[:, None])).astype(jnp.bfloat16)

def coupling(tiles):
    return (tiles[2] * tiles[1] - tiles[3] * tiles[0]) / (tiles[2] * tiles[4] - tiles[3] * tiles[3])

def reference(ldscore, zscores):
    blocks = N_GENOME
    ld_weight = 1.0 / ldscore
    z_float = zscores.astype(jnp.float32)
    z_square = z_float * z_float
    stat_y = lax.optimization_barrier(jnp.sum((z_square * ld_weight[:, None]).reshape(blocks, S_DEV, TRAITS), axis=1))
    stat_l = lax.optimization_barrier(jnp.sum(z_square.reshape(blocks, S_DEV, TRAITS), axis=1))
    stat_inv = lax.optimization_barrier(jnp.sum(ld_weight.reshape(blocks, S_DEV), axis=1))
    stat_ld = lax.optimization_barrier(jnp.sum(ldscore.reshape(blocks, S_DEV), axis=1))
    total_inv = jnp.sum(stat_inv)
    total_ld = jnp.sum(stat_ld)
    total_y = lax.optimization_barrier(jnp.sum(stat_y, axis=0))
    total_l = lax.optimization_barrier(jnp.sum(stat_l, axis=0))
    herit_full = slope_fit(total_inv, total_ld, total_y, total_l, float(S_DEV * blocks))
    herit_del = slope_fit((total_inv - stat_inv)[:, None], (total_ld - stat_ld)[:, None], total_y[None] - stat_y, total_l[None] - stat_l, float(S_DEV * (blocks - 1)))
    herit_pos = jnp.maximum(herit_full, 0.0)
    weight_u = weights_for(herit_pos, ldscore)
    u_float = weight_u.astype(jnp.float32)
    scaled = z_float * u_float
    weighted_z = scaled.astype(jnp.bfloat16)
    weighted_zinv = (scaled * ld_weight[:, None]).astype(jnp.bfloat16)
    weight_inv = (u_float * ld_weight[:, None]).astype(jnp.bfloat16)
    weight_ld = (u_float * ldscore[:, None]).astype(jnp.bfloat16)
    rows_all = jnp.stack([weighted_zinv, weighted_z, weight_inv, weight_u, weight_ld])
    z_cols = weighted_z.astype(jnp.float32).reshape(blocks, S_DEV, TRAITS)
    u_cols = u_float.reshape(blocks, S_DEV, TRAITS)
    herit_floor = jnp.maximum(herit_full, floor_value)
    del_floor = jnp.maximum(herit_del, floor_value)
    row_block = min(256, TRAITS)

    def one_block(start):
        rows = lax.dynamic_slice_in_dim(rows_all, start, row_block, axis=2).astype(jnp.float32)
        rows = rows.reshape(5, blocks, S_DEV, row_block)
        sums = jnp.stack([jnp.einsum('gsi,gsj->gij', rows[0], z_cols), jnp.einsum('gsi,gsj->gij', rows[1], z_cols), jnp.einsum('gsi,gsj->gij', rows[2], u_cols), jnp.einsum('gsi,gsj->gij', rows[3], u_cols), jnp.einsum('gsi,gsj->gij', rows[4], u_cols)])
        tiles = lax.optimization_barrier(sums.astype(jnp.bfloat16)).astype(jnp.float32)
        totals = lax.optimization_barrier(jnp.sum(tiles, axis=1))
        deleted = totals[:, None] - tiles
        full_g = coupling(totals)
        del_g = coupling(deleted)
        rows_full = lax.dynamic_slice_in_dim(herit_floor, start, row_block)
        rows_del = lax.dynamic_slice_in_dim(del_floor, start, row_block, axis=1)
        rg_rows = full_g / jnp.sqrt(rows_full[:, None] * herit_floor[None, :])
        rg_del = del_g / jnp.sqrt(rows_del[:, :, None] * del_floor[:, None, :])
        mean_del = lax.optimization_barrier(jnp.mean(rg_del, axis=0))
        diff = rg_del - mean_del[None]
        spread = lax.optimization_barrier(jnp.sum(diff * diff, axis=0))
        se_rows = jnp.sqrt((blocks - 1) / blocks * spread)
        return (rg_rows, se_rows)
    starts = (jnp.arange(TRAITS // row_block) * row_block).astype(jnp.int32)
    rg_blocks, se_blocks = lax.map(one_block, starts)
    shape = (N_TROW, TRAITS // N_TROW, N_TROW, TRAITS // N_TROW)
    return (rg_blocks.reshape(shape), se_blocks.reshape(shape))
```

```python
import functools

import jax
import jax.numpy as jnp
from jax import lax
from jax.experimental import pallas as pl
from jax.experimental.pallas import tpu as pltpu
from jax.sharding import PartitionSpec as P

floor_value = 0.002
MESH = pl.DeviceIdType.MESH
f32 = jnp.float32
bf16 = jnp.bfloat16

SNP = 1024
TB = 512
LANE = 128
NCH = SNP // LANE
NB = 16
NQ = 4
NX = 4
ROWS = 128
HALF = 256

R_FULL = NB
R_POS = NB + 1
TROWS = 24


def recip(value):
    return 1.0 / value


def column_tile(tile):
    return jnp.transpose(jnp.concatenate([tile] * (LANE // 8), axis=0))


def kernel(
    ld_ref,
    z_ref,
    rg_ref,
    se_ref,
    stage,
    allst,
    ldcol,
    lwcol,
    hrow,
    hdq,
    hdr,
    hdt,
    hcols,
    rbuf,
    cbuf,
    colw,
    lhsy,
    sendy,
    sendx,
    recvy,
    recvx,
    lhsw,
    ucol,
    wbuf,
    wext,
    wfull,
    wfext,
    msend,
    mrecv,
    y_send,
    y_recv,
    g_send,
    g_recv,
    c_send,
    c_recv,
    r_send,
    r_recv,
    a_send,
    a_recv,
    e_send,
    e_recv,
    m_send,
    m_recv,
):
    g = lax.axis_index("genome")
    r = lax.axis_index("trow")
    y = lax.axis_index("tcol")
    zz = g // NX
    x = g % NX
    other = 1 - r
    diag = zz == y
    own_cb = jnp.where(zz > y, other, r)
    half = (x // 2 + r) % 2

    barrier = pltpu.get_barrier_semaphore()

    def greet(dev):
        pl.semaphore_signal(barrier, inc=1, device_id=dev, device_id_type=MESH)

    @pl.loop(1, NB)
    def _(k):
        greet(((g + k) % NB, r, y))

    @pl.loop(1, NQ)
    def _(k):
        greet((g, r, (y + k) % NQ))

    greet((g, other, y))

    @pl.when(diag)
    def _():
        @pl.loop(0, NX)
        def _(k):
            greet((zz * NX + k, other, y))

    @pl.when(jnp.logical_not(diag))
    def _():
        @pl.loop(0, NX)
        def _(k):
            greet((y * NX + k, r, zz))
            greet((y * NX + k, other, zz))

    ld_tile = ld_ref[...]
    ld_t = column_tile(ld_tile)
    for c in range(NCH):
        col = jnp.broadcast_to(ld_t[:, c : c + 1], (LANE, LANE))
        ldcol[c * LANE : (c + 1) * LANE, :] = col
        lwcol[c * LANE : (c + 1) * LANE, :] = recip(col)
    for c in range(TB // LANE):
        lanes = slice(c * LANE, (c + 1) * LANE)
        acc_y = jnp.zeros((8, LANE), f32)
        acc_l = jnp.zeros((8, LANE), f32)
        for s in range(NCH):
            rows = slice(s * LANE, (s + 1) * LANE)
            zraw = z_ref[rows, lanes]
            rbuf[y, c, rows, :] = zraw
            zc = zraw.astype(f32)
            sq = zc * zc
            acc_l = acc_l + jnp.sum(sq.reshape(LANE // 8, 8, LANE), axis=0)
            acc_y = acc_y + jnp.sum((sq * lwcol[rows, :]).reshape(LANE // 8, 8, LANE), axis=0)
        stage[y, c : c + 1, :] = jnp.sum(acc_y, axis=0, keepdims=True)
        stage[y, 4 + c : 5 + c, :] = jnp.sum(acc_l, axis=0, keepdims=True)
    stage[NQ] = ld_tile

    @pl.when(diag)
    def _():
        pl.semaphore_wait(barrier, NB - 1 + NQ - 1 + 1 + NX)

    @pl.when(jnp.logical_not(diag))
    def _():
        pl.semaphore_wait(barrier, NB - 1 + NQ - 1 + 1 + 2 * NX)

    def y_copy(k):
        return pltpu.make_async_remote_copy(
            src_ref=stage.at[y],
            dst_ref=stage.at[y],
            send_sem=y_send.at[k],
            recv_sem=y_recv.at[y],
            device_id=(g, r, (y + k) % NQ),
            device_id_type=MESH,
        )

    @pl.loop(1, NQ)
    def _(k):
        y_copy(k).start()

    def core_copy(src, dst, i):
        return pltpu.make_async_remote_copy(
            src_ref=src,
            dst_ref=dst,
            send_sem=c_send.at[i],
            recv_sem=c_recv.at[i],
            device_id=(g, other, y),
            device_id_type=MESH,
        )

    core_copy(z_ref, cbuf, 0).start()

    def chunk_of(step):
        return (x + 3 * step + 2) % NX

    def row_copy(k, c):
        return pltpu.make_async_remote_copy(
            src_ref=rbuf.at[y, c],
            dst_ref=rbuf.at[y, c],
            send_sem=r_send.at[k, c],
            recv_sem=r_recv.at[y, c],
            device_id=(g, r, (y + k) % NQ),
            device_id_type=MESH,
        )

    @pl.loop(0, NX)
    def _(step):
        @pl.loop(1, NQ)
        def _(k):
            row_copy(k, chunk_of(step)).start()

    @pl.loop(1, NQ)
    def _(k):
        q = (y + k) % NQ
        pltpu.make_async_copy(stage.at[q], stage.at[q], y_recv.at[q]).wait()

    def g_copy(k):
        return pltpu.make_async_remote_copy(
            src_ref=stage,
            dst_ref=allst.at[g],
            send_sem=g_send.at[k],
            recv_sem=g_recv.at[g],
            device_id=((g + k) % NB, r, y),
            device_id_type=MESH,
        )

    @pl.loop(1, NB)
    def _(k):
        g_copy(k).start()

    allst[g] = stage[...]

    @pl.loop(1, NB)
    def _(k):
        b = (g + k) % NB
        pltpu.make_async_copy(allst.at[b], allst.at[b], g_recv.at[b]).wait()

    inv_b = []
    lds_b = []
    for b in range(NB):
        tile = allst[b, NQ]
        inv_b.append(jnp.sum(jnp.sum(recip(tile), axis=0, keepdims=True), axis=1, keepdims=True))
        lds_b.append(jnp.sum(jnp.sum(tile, axis=0, keepdims=True), axis=1, keepdims=True))
    inv_t = functools.reduce(jnp.add, inv_b)
    lds_t = functools.reduce(jnp.add, lds_b)

    def slope(inv, ld, sums, count):
        return (inv * sums[4:8] - count * sums[0:4]) / (inv * ld - count * count)

    n_full = float(SNP * NB)
    n_del = float(SNP * (NB - 1))

    def total_of(q):
        total = allst[0, q]
        for b in range(1, NB):
            total = total + allst[b, q]
        return total

    for q in range(NQ):
        h = jnp.maximum(slope(inv_t, lds_t, total_of(q), n_full), 0.0)
        for c in range(NX):
            hrow[q * NX + c] = h[c : c + 1, :]

    def scaled(h):
        return lax.rsqrt(jnp.maximum(h, floor_value))

    tot_c = total_of(y)
    h_full = slope(inv_t, lds_t, tot_c, n_full)
    hcols[r, TROWS - 8 : TROWS, :] = jnp.zeros((8, TB), f32)
    for c in range(NX):
        lanes = slice(c * LANE, (c + 1) * LANE)
        hcols[r, R_FULL : R_FULL + 1, lanes] = scaled(h_full[c : c + 1, :])
        hcols[r, R_POS : R_POS + 1, lanes] = jnp.maximum(h_full[c : c + 1, :], 0.0)
    for b in range(NB):
        h = scaled(slope(inv_t - inv_b[b], lds_t - lds_b[b], tot_c - allst[b, y], n_del))
        for c in range(NX):
            hcols[r, b : b + 1, c * LANE : (c + 1) * LANE] = h[c : c + 1, :]
    core_copy(hcols.at[r], hcols.at[r], 1).start()

    tot_r = total_of(zz)
    h_full = slope(inv_t, lds_t, tot_r, n_full)
    for c in range(NX):
        hdq[R_FULL, c] = scaled(h_full[c : c + 1, :])
        hdq[R_POS, c] = jnp.maximum(h_full[c : c + 1, :], 0.0)
    for b in range(NB):
        h = scaled(slope(inv_t - inv_b[b], lds_t - lds_b[b], tot_r - allst[b, zz], n_del))
        for c in range(NX):
            hdq[b, c] = h[c : c + 1, :]
    hdr[...] = jnp.zeros((LANE, LANE), f32)
    for b in range(R_POS + 1):
        hdr[b : b + 1, :] = hdq[b, x]
    hdt[...] = jnp.transpose(hdr[...])

    def weigh_columns(src, cb):
        @pl.loop(0, NCH)
        def _(s):
            rows = pl.ds(pl.multiple_of(s * LANE, LANE), LANE)
            for c in range(TB // LANE):
                lanes = slice(c * LANE, (c + 1) * LANE)
                h = hcols[cb, R_POS : R_POS + 1, lanes]
                u = recip(1.0 + h * ldcol[rows, :]).astype(bf16).astype(f32)
                colw[cb, rows, lanes] = (src[rows, lanes].astype(f32) * u).astype(bf16)

    weigh_columns(z_ref, r)
    pltpu.make_async_copy(hcols.at[other], hcols.at[other], c_recv.at[1]).wait()
    pltpu.make_async_copy(cbuf, cbuf, c_recv.at[0]).wait()
    weigh_columns(cbuf, other)

    def pair_copy(q, c):
        return pltpu.make_async_remote_copy(
            src_ref=sendy.at[q * NX + c],
            dst_ref=recvy.at[g],
            send_sem=a_send.at[q * NX + c],
            recv_sem=a_recv.at[g],
            device_id=(q * NX + c, r, y),
            device_id_type=MESH,
        )

    def extra_copy(c):
        return pltpu.make_async_remote_copy(
            src_ref=sendx.at[c],
            dst_ref=recvx.at[g],
            send_sem=e_send.at[c],
            recv_sem=e_recv.at[g],
            device_id=(y * NX + c, r, y),
            device_id_type=MESH,
        )

    def contract(left, right):
        return lax.dot_general(left, right, (((0,), (0,)), ((), ())), preferred_element_type=f32)

    def pair_sums(q, c):
        h = hrow[q * NX + c]
        for s in range(NCH):
            rows = slice(s * LANE, (s + 1) * LANE)
            u = recip(1.0 + h * ldcol[rows, :]).astype(bf16).astype(f32)
            value = rbuf[q, c, rows, :].astype(f32) * u
            lhsy[rows, 0:LANE] = (value * lwcol[rows, :]).astype(bf16)
            lhsy[rows, LANE : 2 * LANE] = value.astype(bf16)
        cb = jnp.where(q > y, other, r)
        sums = contract(lhsy[...], colw[cb]).astype(bf16)
        mine = q * NX + c == g

        @pl.when(mine)
        def _():
            recvy[g, 0] = sums[0:ROWS]
            recvy[g, 1] = sums[ROWS : 2 * ROWS]

        @pl.when(jnp.logical_not(mine))
        def _():
            sendy[q * NX + c, 0] = sums[0:ROWS]
            sendy[q * NX + c, 1] = sums[ROWS : 2 * ROWS]
            pair_copy(q, c).start()

        @pl.when(q == y)
        def _():
            side = (c // 2 + r) % 2
            lanes = pl.ds(pl.multiple_of(side * HALF, HALF), HALF)
            extra = contract(lhsy[...], colw[other, :, lanes]).astype(bf16)

            @pl.when(mine)
            def _():
                recvx[g, 0] = extra[0:ROWS]
                recvx[g, 1] = extra[ROWS : 2 * ROWS]

            @pl.when(jnp.logical_not(mine))
            def _():
                sendx[c, 0] = extra[0:ROWS]
                sendx[c, 1] = extra[ROWS : 2 * ROWS]
                extra_copy(c).start()

    def weight_sums(b):
        tile = allst[b, NQ]
        inv = recip(tile)
        h = hdt[:, R_POS : R_POS + 1]
        for c in range(NCH):
            lanes = slice(c * LANE, (c + 1) * LANE)
            row = tile[c : c + 1, :]
            u16 = recip(1.0 + h * row).astype(bf16)
            u = u16.astype(f32)
            lhsw[0:ROWS, lanes] = (u * inv[c : c + 1, :]).astype(bf16)
            lhsw[ROWS : 2 * ROWS, lanes] = u16
            lhsw[2 * ROWS : 3 * ROWS, lanes] = (u * row).astype(bf16)
        ldc = column_tile(tile)
        h = hcols[own_cb, R_POS : R_POS + 1, :]
        for c in range(NCH):
            ucol[c * LANE : (c + 1) * LANE, :] = recip(1.0 + ldc[:, c : c + 1] * h).astype(bf16)
        wbuf[b] = jnp.dot(lhsw[...], ucol[...], preferred_element_type=f32)

        @pl.when(diag)
        def _():
            lanes = pl.ds(pl.multiple_of(half * HALF, HALF), HALF)
            h = hcols[other, R_POS : R_POS + 1, lanes]
            for c in range(NCH):
                ucol[c * LANE : (c + 1) * LANE, 0:HALF] = recip(1.0 + ldc[:, c : c + 1] * h).astype(
                    bf16
                )
            wext[b] = jnp.dot(lhsw[...], ucol[:, 0:HALF], preferred_element_type=f32)

    @pl.loop(0, NX)
    def _(step):
        c = chunk_of(step)

        @pl.loop(0, NQ)
        def _(k):
            q = (zz + k) % NQ

            @pl.when(q != y)
            def _():
                pltpu.make_async_copy(rbuf.at[q, c], rbuf.at[q, c], r_recv.at[q, c]).wait()

            pair_sums(q, c)

        @pl.loop(0, NB // NX)
        def _(k):
            weight_sums(step * (NB // NX) + k)

    def factors(weights, full, cols, width):
        @pl.loop(0, ROWS // 8)
        def _(t):
            base = pl.multiple_of(t * 8, 8)

            def at(i):
                return pl.ds(i * ROWS + base, 8)

            for c in range(width // LANE):
                lanes = slice(c * LANE, (c + 1) * LANE)
                tot = [weights[0, at(i), lanes] for i in range(3)]
                for b in range(1, NB):
                    tot = [tot[i] + weights[b, at(i), lanes] for i in range(3)]

                def pair(w, b):
                    scale = hdt[pl.ds(base, 8), b : b + 1] * cols(b, c)
                    k = scale / (w[0] * w[2] - w[1] * w[1])
                    return w[0] * k, w[1] * k

                full[0, pl.ds(base, 8), lanes], full[1, pl.ds(base, 8), lanes] = pair(tot, R_FULL)
                for b in range(NB):
                    w = [tot[i] - weights[b, at(i), lanes] for i in range(3)]
                    weights[b, at(0), lanes], weights[b, at(1), lanes] = pair(w, b)

    def own_cols(b, c):
        return hcols[own_cb, b : b + 1, c * LANE : (c + 1) * LANE]

    def extra_cols(b, c):
        lanes = pl.ds(pl.multiple_of(half * HALF + c * LANE, LANE), LANE)
        return hcols[other, b : b + 1, lanes]

    factors(wbuf, wfull, own_cols, TB)

    @pl.when(diag)
    def _():
        factors(wext, wfext, extra_cols, HALF)

    def finish(pairs, weights, full, cb, start, width):
        @pl.loop(0, ROWS // 16)
        def _(t):
            base = pl.multiple_of(t * 16, 16)
            rows = pl.ds(base, 16)
            for c in range(width // LANE):
                lanes = slice(c * LANE, (c + 1) * LANE)
                tot0 = pairs[0, 0, rows, lanes].astype(f32)
                tot1 = pairs[0, 1, rows, lanes].astype(f32)
                for b in range(1, NB):
                    tot0 = tot0 + pairs[b, 0, rows, lanes].astype(f32)
                    tot1 = tot1 + pairs[b, 1, rows, lanes].astype(f32)
                out = pl.ds(pl.multiple_of(start + c * LANE, LANE), LANE)
                rg_ref[cb, rows, out] = full[0, rows, lanes] * tot1 - full[1, rows, lanes] * tot0
                values = []
                for b in range(NB):
                    del0 = tot0 - pairs[b, 0, rows, lanes].astype(f32)
                    del1 = tot1 - pairs[b, 1, rows, lanes].astype(f32)
                    values.append(
                        weights[b, pl.ds(base, 16), lanes] * del1
                        - weights[b, pl.ds(ROWS + base, 16), lanes] * del0
                    )
                mean = functools.reduce(jnp.add, values) * (1.0 / NB)
                spread = functools.reduce(jnp.add, [(v - mean) * (v - mean) for v in values])
                se_ref[cb, rows, out] = jnp.sqrt((NB - 1) / NB * spread)

    @pl.loop(1, NB)
    def _(k):
        b = (g + k) % NB
        pltpu.make_async_copy(recvy.at[b], recvy.at[b], a_recv.at[b]).wait()

    finish(recvy, wbuf, wfull, own_cb, 0, TB)

    @pl.when(diag)
    def _():
        @pl.loop(1, NB)
        def _(k):
            b = (g + k) % NB
            pltpu.make_async_copy(recvx.at[b], recvx.at[b], e_recv.at[b]).wait()

        finish(recvx, wext, wfext, other, half * HALF, HALF)

    def mirror_copy(k):
        dev = (
            jnp.where(diag, zz * NX + k, y * NX + k),
            jnp.where(diag, other, own_cb),
            zz,
        )
        return pltpu.make_async_remote_copy(
            src_ref=msend.at[k],
            dst_ref=mrecv.at[x],
            send_sem=m_send.at[k],
            recv_sem=m_recv.at[x],
            device_id=dev,
            device_id_type=MESH,
        )

    send_first = jnp.where(diag, 2 * half, 0)
    recv_first = jnp.where(diag, 2 * (1 - half), 0)
    pieces = jnp.where(diag, 2, NX)
    send_cb = jnp.where(diag, other, own_cb)
    recv_cb = jnp.where(diag, other, 1 - own_cb)

    @pl.loop(0, pieces)
    def _(i):
        k = send_first + i
        lanes = pl.ds(pl.multiple_of(k * LANE, LANE), LANE)
        msend[k, 0] = jnp.transpose(rg_ref[send_cb, :, lanes]).astype(bf16)
        msend[k, 1] = jnp.transpose(se_ref[send_cb, :, lanes]).astype(bf16)
        mirror_copy(k).start()

    @pl.loop(0, pieces)
    def _(i):
        k = recv_first + i
        lanes = pl.ds(pl.multiple_of(k * LANE, LANE), LANE)
        pltpu.make_async_copy(mrecv.at[k], mrecv.at[k], m_recv.at[k]).wait()
        rg_ref[recv_cb, :, lanes] = mrecv[k, 0].astype(f32)
        se_ref[recv_cb, :, lanes] = mrecv[k, 1].astype(f32)

    @pl.loop(1, NQ)
    def _(k):
        y_copy(k).wait_send()

        @pl.loop(0, NX)
        def _(c):
            row_copy(k, c).wait_send()

    core_copy(z_ref, cbuf, 0).wait_send()
    core_copy(hcols.at[r], hcols.at[r], 1).wait_send()

    @pl.loop(1, NB)
    def _(k):
        g_copy(k).wait_send()
        p = (g + k) % NB
        pair_copy(p // NX, p % NX).wait_send()

    @pl.loop(0, NX)
    def _(c):
        @pl.when(y * NX + c != g)
        def _():
            extra_copy(c).wait_send()

    @pl.loop(0, pieces)
    def _(i):
        mirror_copy(send_first + i).wait_send()


def per_device(ldscore, zscores):
    dma = pltpu.SemaphoreType.DMA
    out = jax.ShapeDtypeStruct((2, ROWS, TB), f32)
    rg, se = pl.pallas_call(
        kernel,
        out_shape=(out, out),
        in_specs=[pl.BlockSpec(memory_space=pltpu.VMEM)] * 2,
        out_specs=[pl.BlockSpec(memory_space=pltpu.VMEM)] * 2,
        scratch_shapes=[
            pltpu.VMEM((NQ + 1, 8, LANE), f32),
            pltpu.VMEM((NB, NQ + 1, 8, LANE), f32),
            pltpu.VMEM((SNP, LANE), f32),
            pltpu.VMEM((SNP, LANE), f32),
            pltpu.VMEM((NQ * NX, 1, LANE), f32),
            pltpu.VMEM((R_POS + 1, NX, 1, LANE), f32),
            pltpu.VMEM((LANE, LANE), f32),
            pltpu.VMEM((LANE, LANE), f32),
            pltpu.VMEM((2, TROWS, TB), f32),
            pltpu.VMEM((NQ, NX, SNP, LANE), bf16),
            pltpu.VMEM((SNP, TB), bf16),
            pltpu.VMEM((2, SNP, TB), bf16),
            pltpu.VMEM((SNP, 2 * LANE), bf16),
            pltpu.VMEM((NB, 2, ROWS, TB), bf16),
            pltpu.VMEM((NX, 2, ROWS, HALF), bf16),
            pltpu.VMEM((NB, 2, ROWS, TB), bf16),
            pltpu.VMEM((NB, 2, ROWS, HALF), bf16),
            pltpu.VMEM((3 * ROWS, SNP), bf16),
            pltpu.VMEM((SNP, TB), bf16),
            pltpu.VMEM((NB, 3 * ROWS, TB), f32),
            pltpu.VMEM((NB, 3 * ROWS, HALF), f32),
            pltpu.VMEM((2, ROWS, TB), f32),
            pltpu.VMEM((2, ROWS, HALF), f32),
            pltpu.VMEM((NX, 2, LANE, LANE), bf16),
            pltpu.VMEM((NX, 2, LANE, LANE), bf16),
            dma((NQ,)),
            dma((NQ,)),
            dma((NB,)),
            dma((NB,)),
            dma((2,)),
            dma((2,)),
            dma((NQ, NX)),
            dma((NQ, NX)),
            dma((NB,)),
            dma((NB,)),
            dma((NX,)),
            dma((NB,)),
            dma((NX,)),
            dma((NX,)),
        ],
        compiler_params=pltpu.CompilerParams(
            collective_id=0, has_side_effects=True, vmem_limit_bytes=56 * 1024 * 1024
        ),
    )(ldscore.reshape(8, LANE), zscores)
    return (rg.transpose(1, 0, 2)[None], se.transpose(1, 0, 2)[None])


def solution(mesh):
    return jax.shard_map(
        per_device,
        mesh=mesh,
        in_specs=(P("genome"), P("genome", ("trow", "tcol"))),
        out_specs=(P("trow", "genome", None, "tcol"), P("trow", "genome", None, "tcol")),
        check_vma=False,
    )
```

```python
import functools

import jax
import jax.numpy as jnp
from jax import lax
from jax.experimental import pallas as pl
from jax.experimental.pallas import tpu as pltpu
from jax.sharding import PartitionSpec as P

floor_value = 0.002
MESH = pl.DeviceIdType.MESH
f32 = jnp.float32
bf16 = jnp.bfloat16

SNP = 1024
TB = 512
LANE = 128
NCH = SNP // LANE
NB = 16
NQ = 4
NX = 4
ROWS = 128
HALF = 256

R_FULL = NB
R_POS = NB + 1
TROWS = 24

T_OTHER = NQ
T_LD = NQ + 1


def recip(value):
    return 1.0 / value


def column_tile(tile):
    return jnp.transpose(jnp.concatenate([tile] * (LANE // 8), axis=0))


def kernel(
    ld_ref,
    z_ref,
    rg_ref,
    se_ref,
    stage,
    allst,
    ldcol,
    lwcol,
    hrow,
    hdq,
    hdr,
    hdt,
    hcols,
    ctab,
    rbuf,
    cbuf,
    colw,
    lhsy,
    sendy,
    sendx,
    recvy,
    recvx,
    lhsw,
    ucol,
    wbuf,
    wext,
    wfull,
    wfext,
    msend,
    mrecv,
    y_send,
    y_recv,
    g_send,
    g_recv,
    c_send,
    c_recv,
    r_send,
    r_recv,
    f_send,
    f_recv,
    a_send,
    a_recv,
    e_send,
    e_recv,
    m_send,
    m_recv,
):
    g = lax.axis_index("genome")
    r = lax.axis_index("trow")
    y = lax.axis_index("tcol")
    zz = g // NX
    x = g % NX
    other = 1 - r
    diag = zz == y
    own_cb = jnp.where(zz > y, other, r)
    half = (x // 2 + r) % 2
    fifth = jnp.logical_and(diag, x < 2)

    barrier = pltpu.get_barrier_semaphore()

    def greet(dev):
        pl.semaphore_signal(barrier, inc=1, device_id=dev, device_id_type=MESH)

    @pl.loop(1, NB)
    def _(k):
        greet(((g + k) % NB, r, y))

    @pl.loop(1, NQ)
    def _(k):
        greet((g, r, (y + k) % NQ))

    greet((g, other, y))

    @pl.when(diag)
    def _():
        @pl.loop(0, NX)
        def _(k):
            greet((zz * NX + k, other, y))

    @pl.when(jnp.logical_not(diag))
    def _():
        @pl.loop(0, NX)
        def _(k):
            greet((y * NX + k, r, zz))
            greet((y * NX + k, other, zz))

    ld_tile = ld_ref[...]
    ld_t = column_tile(ld_tile)
    for c in range(NCH):
        col = jnp.broadcast_to(ld_t[:, c : c + 1], (LANE, LANE))
        ldcol[c * LANE : (c + 1) * LANE, :] = col
        lwcol[c * LANE : (c + 1) * LANE, :] = recip(col)
    for c in range(TB // LANE):
        lanes = slice(c * LANE, (c + 1) * LANE)
        acc_y = jnp.zeros((8, LANE), f32)
        acc_l = jnp.zeros((8, LANE), f32)
        for s in range(NCH):
            rows = slice(s * LANE, (s + 1) * LANE)
            zraw = z_ref[rows, lanes]
            rbuf[y, c, rows, :] = zraw
            zc = zraw.astype(f32)
            sq = zc * zc
            acc_l = acc_l + jnp.sum(sq.reshape(LANE // 8, 8, LANE), axis=0)
            acc_y = acc_y + jnp.sum((sq * lwcol[rows, :]).reshape(LANE // 8, 8, LANE), axis=0)
        stage[y, c : c + 1, :] = jnp.sum(acc_y, axis=0, keepdims=True)
        stage[y, 4 + c : 5 + c, :] = jnp.sum(acc_l, axis=0, keepdims=True)
    stage[T_LD] = ld_tile

    @pl.when(diag)
    def _():
        pl.semaphore_wait(barrier, NB - 1 + NQ - 1 + 1 + NX)

    @pl.when(jnp.logical_not(diag))
    def _():
        pl.semaphore_wait(barrier, NB - 1 + NQ - 1 + 1 + 2 * NX)

    def y_copy(k):
        return pltpu.make_async_remote_copy(
            src_ref=stage.at[y],
            dst_ref=stage.at[y],
            send_sem=y_send.at[k],
            recv_sem=y_recv.at[y],
            device_id=(g, r, (y + k) % NQ),
            device_id_type=MESH,
        )

    def core_copy(src, dst, i):
        return pltpu.make_async_remote_copy(
            src_ref=src,
            dst_ref=dst,
            send_sem=c_send.at[i],
            recv_sem=c_recv.at[i],
            device_id=(g, other, y),
            device_id_type=MESH,
        )

    @pl.loop(1, NQ)
    def _(k):
        y_copy(k).start()

    core_copy(stage.at[y], stage.at[T_OTHER], 0).start()
    core_copy(z_ref, cbuf, 1).start()

    def chunk_of(step):
        return (x + 3 * step + 2) % NX

    def row_copy(way, c):
        return pltpu.make_async_remote_copy(
            src_ref=rbuf.at[y, c],
            dst_ref=rbuf.at[y, c],
            send_sem=r_send.at[way, c],
            recv_sem=r_recv.at[way, c],
            device_id=(g, r, (y + 1 + 2 * way) % NQ),
            device_id_type=MESH,
        )

    def far_copy(way, c):
        q = (y + 3 + 2 * way) % NQ
        part = rbuf.at[q, c, pl.ds(pl.multiple_of(way * (SNP // 2), SNP // 2), SNP // 2)]
        return pltpu.make_async_remote_copy(
            src_ref=part,
            dst_ref=part,
            send_sem=f_send.at[way, c],
            recv_sem=f_recv.at[way, c],
            device_id=(g, r, (y + 1 + 2 * way) % NQ),
            device_id_type=MESH,
        )

    def send_chunk(step):
        c = chunk_of(step)
        row_copy(0, c).start()
        row_copy(1, c).start()

    def pass_on(step):
        c = chunk_of(step)
        for way in range(2):
            q = (y + 3 + 2 * way) % NQ
            pltpu.make_async_copy(rbuf.at[q, c], rbuf.at[q, c], r_recv.at[way, c]).wait()
            far_copy(way, c).start()

    send_chunk(0)
    send_chunk(1)

    @pl.loop(1, NQ)
    def _(k):
        q = (y + k) % NQ
        pltpu.make_async_copy(stage.at[q], stage.at[q], y_recv.at[q]).wait()

    pltpu.make_async_copy(stage.at[T_OTHER], stage.at[T_OTHER], c_recv.at[0]).wait()

    def g_copy(k):
        return pltpu.make_async_remote_copy(
            src_ref=stage,
            dst_ref=allst.at[g],
            send_sem=g_send.at[k],
            recv_sem=g_recv.at[g],
            device_id=((g + k) % NB, r, y),
            device_id_type=MESH,
        )

    @pl.loop(1, NB)
    def _(k):
        g_copy(k).start()

    allst[g] = stage[...]

    @pl.loop(1, NB)
    def _(k):
        b = (g + k) % NB
        pltpu.make_async_copy(allst.at[b], allst.at[b], g_recv.at[b]).wait()

    inv_b = []
    lds_b = []
    for b in range(NB):
        tile = allst[b, T_LD]
        inv_b.append(jnp.sum(jnp.sum(recip(tile), axis=0, keepdims=True), axis=1, keepdims=True))
        lds_b.append(jnp.sum(jnp.sum(tile, axis=0, keepdims=True), axis=1, keepdims=True))
    inv_t = functools.reduce(jnp.add, inv_b)
    lds_t = functools.reduce(jnp.add, lds_b)

    def slope(inv, ld, sums, count):
        return (inv * sums[4:8] - count * sums[0:4]) / (inv * ld - count * count)

    n_full = float(SNP * NB)
    n_del = float(SNP * (NB - 1))

    def total_of(q):
        total = allst[0, q]
        for b in range(1, NB):
            total = total + allst[b, q]
        return total

    def scaled(h):
        return lax.rsqrt(jnp.maximum(h, floor_value))

    for q in range(NQ):
        h = jnp.maximum(slope(inv_t, lds_t, total_of(q), n_full), 0.0)
        for c in range(NX):
            hrow[q * NX + c] = h[c : c + 1, :]

    for cb, q in ((r, y), (other, T_OTHER)):
        h_full = slope(inv_t, lds_t, total_of(q), n_full)
        hcols[cb, TROWS - 8 : TROWS, :] = jnp.zeros((8, TB), f32)
        for c in range(NX):
            lanes = slice(c * LANE, (c + 1) * LANE)
            hcols[cb, R_FULL : R_FULL + 1, lanes] = scaled(h_full[c : c + 1, :])
            hcols[cb, R_POS : R_POS + 1, lanes] = jnp.maximum(h_full[c : c + 1, :], 0.0)

    def weigh_columns(src, cb):
        @pl.loop(0, NCH)
        def _(s):
            rows = pl.ds(pl.multiple_of(s * LANE, LANE), LANE)
            for c in range(TB // LANE):
                lanes = slice(c * LANE, (c + 1) * LANE)
                h = hcols[cb, R_POS : R_POS + 1, lanes]
                u = recip(1.0 + h * ldcol[rows, :]).astype(bf16).astype(f32)
                colw[cb, rows, lanes] = (src[rows, lanes].astype(f32) * u).astype(bf16)

    weigh_columns(z_ref, r)
    pltpu.make_async_copy(cbuf, cbuf, c_recv.at[1]).wait()
    weigh_columns(cbuf, other)

    pass_on(0)
    send_chunk(2)

    def pair_copy(q, c):
        return pltpu.make_async_remote_copy(
            src_ref=sendy.at[q * NX + c],
            dst_ref=recvy.at[g],
            send_sem=a_send.at[q * NX + c],
            recv_sem=a_recv.at[g],
            device_id=(q * NX + c, r, y),
            device_id_type=MESH,
        )

    def extra_copy(c):
        return pltpu.make_async_remote_copy(
            src_ref=sendx.at[c],
            dst_ref=recvx.at[g],
            send_sem=e_send.at[c],
            recv_sem=e_recv.at[g],
            device_id=(y * NX + c, r, y),
            device_id_type=MESH,
        )

    def contract(left, right):
        return lax.dot_general(left, right, (((0,), (0,)), ((), ())), preferred_element_type=f32)

    def chunk_lanes(c):
        return pl.ds(pl.multiple_of((c % NX) * LANE, LANE), LANE)

    def half_lanes(side):
        return pl.ds(pl.multiple_of(side * HALF, HALF), HALF)

    def weigh_rows(q, c):
        h = hrow[q * NX + c]
        for s in range(NCH):
            rows = slice(s * LANE, (s + 1) * LANE)
            u = recip(1.0 + h * ldcol[rows, :]).astype(bf16).astype(f32)
            value = rbuf[q, c, rows, :].astype(f32) * u
            lhsy[rows, 0:LANE] = (value * lwcol[rows, :]).astype(bf16)
            lhsy[rows, LANE : 2 * LANE] = value.astype(bf16)

    def deliver(sums, q, c, send, recv, slot, copy):
        mine = q * NX + c == g

        @pl.when(mine)
        def _():
            recv[g, 0] = sums[0:ROWS]
            recv[g, 1] = sums[ROWS : 2 * ROWS]

        @pl.when(jnp.logical_not(mine))
        def _():
            send[slot, 0] = sums[0:ROWS]
            send[slot, 1] = sums[ROWS : 2 * ROWS]
            copy.start()

    def pair_sums(q, c):
        weigh_rows(q, c)
        cb = jnp.where(q > y, other, r)
        sums = contract(lhsy[...], colw[cb]).astype(bf16)
        deliver(sums, q, c, sendy, recvy, q * NX + c, pair_copy(q, c))

    def own_sums(c):
        weigh_rows(y, c)
        cols = jnp.concatenate(
            [
                colw[other, :, half_lanes((c // 2 + r) % 2)],
                colw[r, :, chunk_lanes(c)],
                colw[r, :, chunk_lanes(c + 1)],
            ],
            axis=1,
        )
        sums = contract(lhsy[...], cols).astype(bf16)
        deliver(sums, y, c, sendy, recvy, y * NX + c, pair_copy(y, c))

        @pl.when(c < 2)
        def _():
            extra = contract(lhsy[...], colw[r, :, chunk_lanes(c + 2)]).astype(bf16)
            deliver(extra, y, c, sendx, recvx, c, extra_copy(c))

    @pl.loop(0, NX)
    def _(step):
        own_sums(chunk_of(step))

    def make_table(rows):
        @pl.when(jnp.logical_not(diag))
        def _():
            ctab[rows, 0:TB] = hcols[own_cb, rows, :]
            ctab[rows, TB : TB + LANE] = hcols[own_cb, rows, 0:LANE]

        @pl.when(diag)
        def _():
            ctab[rows, 0:HALF] = hcols[other, rows, half_lanes(half)]
            for i in range(3):
                ctab[rows, HALF + i * LANE : HALF + (i + 1) * LANE] = hcols[
                    r, rows, chunk_lanes(x + i)
                ]

    make_table(slice(TROWS - 8, TROWS))
    hdr[...] = jnp.zeros((LANE, LANE), f32)
    hdr[R_POS : R_POS + 1, :] = hrow[zz * NX + x]
    hdt[...] = jnp.transpose(hdr[...])

    def weight_sums(b):
        tile = allst[b, T_LD]
        inv = recip(tile)
        h = hdt[:, R_POS : R_POS + 1]
        for c in range(NCH):
            lanes = slice(c * LANE, (c + 1) * LANE)
            row = tile[c : c + 1, :]
            u16 = recip(1.0 + h * row).astype(bf16)
            u = u16.astype(f32)
            lhsw[0:ROWS, lanes] = (u * inv[c : c + 1, :]).astype(bf16)
            lhsw[ROWS : 2 * ROWS, lanes] = u16
            lhsw[2 * ROWS : 3 * ROWS, lanes] = (u * row).astype(bf16)
        ldc = column_tile(tile)
        h = ctab[R_POS : R_POS + 1, 0:TB]
        for c in range(NCH):
            ucol[c * LANE : (c + 1) * LANE, :] = recip(1.0 + ldc[:, c : c + 1] * h).astype(bf16)
        wbuf[b] = jnp.dot(lhsw[...], ucol[...], preferred_element_type=f32)

        @pl.when(fifth)
        def _():
            h = ctab[R_POS : R_POS + 1, TB : TB + LANE]
            for c in range(NCH):
                ucol[c * LANE : (c + 1) * LANE, 0:LANE] = recip(1.0 + ldc[:, c : c + 1] * h).astype(
                    bf16
                )
            wext[b] = jnp.dot(lhsw[...], ucol[:, 0:LANE], preferred_element_type=f32)

    @pl.loop(0, NX)
    def _(step):
        @pl.when(step < NX - 1)
        def _():
            pass_on(step + 1)

        @pl.when(step == 0)
        def _():
            send_chunk(NX - 1)

        c = chunk_of(step)
        far = (y + 2) % NQ
        for way in range(2):
            part = rbuf.at[far, c, pl.ds(way * (SNP // 2), SNP // 2)]
            pltpu.make_async_copy(part, part, f_recv.at[way, c]).wait()

        @pl.loop(1, NQ)
        def _(k):
            pair_sums((y + k) % NQ, c)

        @pl.loop(0, NB // NX)
        def _(k):
            weight_sums(step * (NB // NX) + k)

    for cb, q in ((r, y), (other, T_OTHER)):
        total = total_of(q)
        for b in range(NB):
            h = scaled(slope(inv_t - inv_b[b], lds_t - lds_b[b], total - allst[b, q], n_del))
            for c in range(NX):
                hcols[cb, b : b + 1, c * LANE : (c + 1) * LANE] = h[c : c + 1, :]
    make_table(slice(0, NB))
    total = total_of(zz)
    h_full = scaled(slope(inv_t, lds_t, total, n_full))
    for c in range(NX):
        hdq[R_FULL, c] = h_full[c : c + 1, :]
    for b in range(NB):
        h = scaled(slope(inv_t - inv_b[b], lds_t - lds_b[b], total - allst[b, zz], n_del))
        for c in range(NX):
            hdq[b, c] = h[c : c + 1, :]
    for b in range(NB + 1):
        hdr[b : b + 1, :] = hdq[b, x]
    hdt[...] = jnp.transpose(hdr[...])

    def factors(weights, full, first, width):
        @pl.loop(0, ROWS // 8)
        def _(t):
            base = pl.multiple_of(t * 8, 8)

            def at(i):
                return pl.ds(i * ROWS + base, 8)

            for c in range(width // LANE):
                lanes = slice(c * LANE, (c + 1) * LANE)
                tlanes = slice(first + c * LANE, first + (c + 1) * LANE)
                tot = [weights[0, at(i), lanes] for i in range(3)]
                for b in range(1, NB):
                    tot = [tot[i] + weights[b, at(i), lanes] for i in range(3)]

                def pair(w, b):
                    scale = hdt[pl.ds(base, 8), b : b + 1] * ctab[b : b + 1, tlanes]
                    k = scale / (w[0] * w[2] - w[1] * w[1])
                    return w[0] * k, w[1] * k

                full[0, pl.ds(base, 8), lanes], full[1, pl.ds(base, 8), lanes] = pair(tot, R_FULL)
                for b in range(NB):
                    w = [tot[i] - weights[b, at(i), lanes] for i in range(3)]
                    weights[b, at(0), lanes], weights[b, at(1), lanes] = pair(w, b)

    factors(wbuf, wfull, 0, TB)

    @pl.when(fifth)
    def _():
        factors(wext, wfext, TB, LANE)

    def place(j):
        on_half = j < 2
        cb = jnp.where(jnp.logical_not(diag), own_cb, jnp.where(on_half, other, r))
        chunk = jnp.where(
            jnp.logical_not(diag), j, jnp.where(on_half, 2 * half + j, (x + j + 2) % NX)
        )
        return cb, chunk

    def mirror_copy(j):
        cb, chunk = place(j)
        slot = jnp.where(jnp.logical_and(diag, j >= 2), j + 1, x)
        return pltpu.make_async_remote_copy(
            src_ref=msend.at[j],
            dst_ref=mrecv.at[slot],
            send_sem=m_send.at[j],
            recv_sem=m_recv.at[slot],
            device_id=(y * NX + chunk, cb, zz),
            device_id_type=MESH,
        )

    def sends(j):
        return jnp.logical_not(jnp.logical_and(diag, j == 2))

    def finish(pairs, weights, full, j, first):
        cb, chunk = place(j)
        out = chunk_lanes(chunk)
        lanes = pl.ds(pl.multiple_of(first, LANE), LANE)

        @pl.loop(0, ROWS // 16)
        def _(t):
            base = pl.multiple_of(t * 16, 16)
            rows = pl.ds(base, 16)
            tot0 = pairs[0, 0, rows, lanes].astype(f32)
            tot1 = pairs[0, 1, rows, lanes].astype(f32)
            for b in range(1, NB):
                tot0 = tot0 + pairs[b, 0, rows, lanes].astype(f32)
                tot1 = tot1 + pairs[b, 1, rows, lanes].astype(f32)
            rg_ref[cb, rows, out] = full[0, rows, lanes] * tot1 - full[1, rows, lanes] * tot0
            values = []
            for b in range(NB):
                del0 = tot0 - pairs[b, 0, rows, lanes].astype(f32)
                del1 = tot1 - pairs[b, 1, rows, lanes].astype(f32)
                values.append(
                    weights[b, pl.ds(base, 16), lanes] * del1
                    - weights[b, pl.ds(ROWS + base, 16), lanes] * del0
                )
            mean = functools.reduce(jnp.add, values) * (1.0 / NB)
            spread = functools.reduce(jnp.add, [(v - mean) * (v - mean) for v in values])
            se_ref[cb, rows, out] = jnp.sqrt((NB - 1) / NB * spread)

        @pl.when(sends(j))
        def _():
            msend[j, 0] = jnp.transpose(rg_ref[cb, :, out]).astype(bf16)
            msend[j, 1] = jnp.transpose(se_ref[cb, :, out]).astype(bf16)
            mirror_copy(j).start()

    @pl.loop(1, NB)
    def _(k):
        b = (g + k) % NB
        pltpu.make_async_copy(recvy.at[b], recvy.at[b], a_recv.at[b]).wait()

    @pl.loop(0, NX)
    def _(j):
        finish(recvy, wbuf, wfull, j, j * LANE)

    @pl.when(fifth)
    def _():
        @pl.loop(1, NB)
        def _(k):
            b = (g + k) % NB
            pltpu.make_async_copy(recvx.at[b], recvx.at[b], e_recv.at[b]).wait()

        finish(recvx, wext, wfext, NX, 0)

    def take(slot, cb, chunk):
        pltpu.make_async_copy(mrecv.at[slot], mrecv.at[slot], m_recv.at[slot]).wait()
        rg_ref[cb, :, chunk_lanes(chunk)] = mrecv[slot, 0].astype(f32)
        se_ref[cb, :, chunk_lanes(chunk)] = mrecv[slot, 1].astype(f32)

    @pl.when(jnp.logical_not(diag))
    def _():
        @pl.loop(0, NX)
        def _(k):
            take(k, 1 - own_cb, k)

    @pl.when(diag)
    def _():
        @pl.loop(0, 2)
        def _(k):
            chunk = 2 * (1 - half) + k
            take(chunk, other, chunk)

        take(NX, r, x + 3)

        @pl.when(x >= 2)
        def _():
            take(NX + 1, r, x + 2)

    @pl.loop(1, NQ)
    def _(k):
        y_copy(k).wait_send()

    core_copy(stage.at[y], stage.at[T_OTHER], 0).wait_send()
    core_copy(z_ref, cbuf, 1).wait_send()

    @pl.loop(0, NX)
    def _(c):
        for way in range(2):
            row_copy(way, c).wait_send()
            far_copy(way, c).wait_send()

    @pl.loop(1, NB)
    def _(k):
        g_copy(k).wait_send()
        p = (g + k) % NB
        pair_copy(p // NX, p % NX).wait_send()

    @pl.loop(0, 2)
    def _(c):
        @pl.when(y * NX + c != g)
        def _():
            extra_copy(c).wait_send()

    @pl.loop(0, NX)
    def _(j):
        @pl.when(sends(j))
        def _():
            mirror_copy(j).wait_send()

    @pl.when(fifth)
    def _():
        mirror_copy(NX).wait_send()


def per_device(ldscore, zscores):
    dma = pltpu.SemaphoreType.DMA
    out = jax.ShapeDtypeStruct((2, ROWS, TB), f32)
    rg, se = pl.pallas_call(
        kernel,
        out_shape=(out, out),
        in_specs=[pl.BlockSpec(memory_space=pltpu.VMEM)] * 2,
        out_specs=[pl.BlockSpec(memory_space=pltpu.VMEM)] * 2,
        scratch_shapes=[
            pltpu.VMEM((T_LD + 1, 8, LANE), f32),
            pltpu.VMEM((NB, T_LD + 1, 8, LANE), f32),
            pltpu.VMEM((SNP, LANE), f32),
            pltpu.VMEM((SNP, LANE), f32),
            pltpu.VMEM((NQ * NX, 1, LANE), f32),
            pltpu.VMEM((R_POS + 1, NX, 1, LANE), f32),
            pltpu.VMEM((LANE, LANE), f32),
            pltpu.VMEM((LANE, LANE), f32),
            pltpu.VMEM((2, TROWS, TB), f32),
            pltpu.VMEM((TROWS, TB + LANE), f32),
            pltpu.VMEM((NQ, NX, SNP, LANE), bf16),
            pltpu.VMEM((SNP, TB), bf16),
            pltpu.VMEM((2, SNP, TB), bf16),
            pltpu.VMEM((SNP, 2 * LANE), bf16),
            pltpu.VMEM((NB, 2, ROWS, TB), bf16),
            pltpu.VMEM((2, 2, ROWS, LANE), bf16),
            pltpu.VMEM((NB, 2, ROWS, TB), bf16),
            pltpu.VMEM((NB, 2, ROWS, LANE), bf16),
            pltpu.VMEM((3 * ROWS, SNP), bf16),
            pltpu.VMEM((SNP, TB), bf16),
            pltpu.VMEM((NB, 3 * ROWS, TB), f32),
            pltpu.VMEM((NB, 3 * ROWS, LANE), f32),
            pltpu.VMEM((2, ROWS, TB), f32),
            pltpu.VMEM((2, ROWS, LANE), f32),
            pltpu.VMEM((NX + 1, 2, LANE, LANE), bf16),
            pltpu.VMEM((NX + 2, 2, LANE, LANE), bf16),
            dma((NQ,)),
            dma((NQ,)),
            dma((NB,)),
            dma((NB,)),
            dma((2,)),
            dma((2,)),
            dma((2, NX)),
            dma((2, NX)),
            dma((2, NX)),
            dma((2, NX)),
            dma((NB,)),
            dma((NB,)),
            dma((2,)),
            dma((NB,)),
            dma((NX + 1,)),
            dma((NX + 2,)),
        ],
        compiler_params=pltpu.CompilerParams(
            collective_id=0, has_side_effects=True, vmem_limit_bytes=56 * 1024 * 1024
        ),
    )(ldscore.reshape(8, LANE), zscores)
    return (rg.transpose(1, 0, 2)[None], se.transpose(1, 0, 2)[None])


def solution(mesh):
    return jax.shard_map(
        per_device,
        mesh=mesh,
        in_specs=(P("genome"), P("genome", ("trow", "tcol"))),
        out_specs=(P("trow", "genome", None, "tcol"), P("trow", "genome", None, "tcol")),
        check_vma=False,
    )
```

```python
import functools

import jax
import jax.numpy as jnp
from jax import lax
from jax.experimental import pallas as pl
from jax.experimental.pallas import tpu as pltpu
from jax.sharding import PartitionSpec as P

floor_value = 0.002
MESH = pl.DeviceIdType.MESH
f32 = jnp.float32
bf16 = jnp.bfloat16

SNP = 1024
TB = 512
LANE = 128
NCH = SNP // LANE
NB = 16
NQ = 4
NX = 4
ROWS = 128
HALF = 256

R_FULL = NB
R_POS = NB + 1
TROWS = 24

T_OTHER = NQ
T_LD = NQ + 1

W_STEP = 3

NT = 4
PART = ROWS // NT
ORDER = (
    (2, 2), (1, 1), (3, 3), (1, 3), (3, 1), (1, 2), (3, 2), (2, 1), (2, 3),
    (0, 1), (1, 0), (0, 3), (3, 0), (0, 2), (2, 0),
)


def recip(value):
    return 1.0 / value


def column_tile(tile):
    return jnp.transpose(jnp.concatenate([tile] * (LANE // 8), axis=0))


def kernel(
    ld_ref,
    z_ref,
    rg_ref,
    se_ref,
    stage,
    allst,
    ldcol,
    lwcol,
    hrow,
    hpos,
    hdq,
    hdr,
    hdt,
    hcols,
    ctab,
    rbuf,
    cbuf,
    colw,
    lhsy,
    sendy,
    sendx,
    recvy,
    recvx,
    lhsw,
    ucol,
    wbuf,
    wext,
    wfull,
    wfext,
    msend,
    mrecv,
    y_send,
    y_recv,
    g_send,
    g_recv,
    c_send,
    c_recv,
    r_send,
    r_recv,
    f_send,
    f_recv,
    a_send,
    a_recv,
    e_send,
    e_recv,
    m_send,
    m_recv,
):
    g = lax.axis_index("genome")
    r = lax.axis_index("trow")
    y = lax.axis_index("tcol")
    zz = g // NX
    x = g % NX
    other = 1 - r
    diag = zz == y
    own_cb = jnp.where(zz > y, other, r)
    half = (x // 2 + r) % 2
    fifth = jnp.logical_and(diag, x < 2)

    barrier = pltpu.get_barrier_semaphore()

    def greet(dev):
        pl.semaphore_signal(barrier, inc=1, device_id=dev, device_id_type=MESH)

    @pl.loop(1, NB)
    def _(k):
        greet(((g + k) % NB, r, y))

    @pl.loop(1, NQ)
    def _(k):
        greet((g, r, (y + k) % NQ))

    greet((g, other, y))

    @pl.when(diag)
    def _():
        @pl.loop(0, NX)
        def _(k):
            greet((zz * NX + k, other, y))

    @pl.when(jnp.logical_not(diag))
    def _():
        @pl.loop(0, NX)
        def _(k):
            greet((y * NX + k, r, zz))
            greet((y * NX + k, other, zz))

    ld_tile = ld_ref[...]
    ld_t = column_tile(ld_tile)
    for c in range(NCH):
        col = jnp.broadcast_to(ld_t[:, c : c + 1], (LANE, LANE))
        ldcol[c * LANE : (c + 1) * LANE, :] = col
        lwcol[c * LANE : (c + 1) * LANE, :] = recip(col)
    for c in range(TB // LANE):
        lanes = slice(c * LANE, (c + 1) * LANE)
        acc_y = jnp.zeros((8, LANE), f32)
        acc_l = jnp.zeros((8, LANE), f32)
        for s in range(NCH):
            rows = slice(s * LANE, (s + 1) * LANE)
            zc = z_ref[rows, lanes].astype(f32)
            sq = zc * zc
            acc_l = acc_l + jnp.sum(sq.reshape(LANE // 8, 8, LANE), axis=0)
            acc_y = acc_y + jnp.sum((sq * lwcol[rows, :]).reshape(LANE // 8, 8, LANE), axis=0)
        stage[y, c : c + 1, :] = jnp.sum(acc_y, axis=0, keepdims=True)
        stage[y, 4 + c : 5 + c, :] = jnp.sum(acc_l, axis=0, keepdims=True)
    stage[T_LD] = ld_tile

    def gather_parts(value, t):
        return jnp.concatenate(
            [value[:, c * LANE + t * PART : c * LANE + (t + 1) * PART] for c in range(NX)], axis=1
        )

    def make_chunk(t):
        for s in range(NCH):
            rows = slice(s * LANE, (s + 1) * LANE)
            rbuf[y, t, rows, :] = gather_parts(z_ref[rows, :], t)

    make_chunk(0)

    @pl.when(diag)
    def _():
        pl.semaphore_wait(barrier, NB - 1 + NQ - 1 + 1 + NX)

    @pl.when(jnp.logical_not(diag))
    def _():
        pl.semaphore_wait(barrier, NB - 1 + NQ - 1 + 1 + 2 * NX)

    def y_copy(k):
        return pltpu.make_async_remote_copy(
            src_ref=stage.at[y],
            dst_ref=stage.at[y],
            send_sem=y_send.at[k],
            recv_sem=y_recv.at[y],
            device_id=(g, r, (y + k) % NQ),
            device_id_type=MESH,
        )

    def core_copy(src, dst, i):
        return pltpu.make_async_remote_copy(
            src_ref=src,
            dst_ref=dst,
            send_sem=c_send.at[i],
            recv_sem=c_recv.at[i],
            device_id=(g, other, y),
            device_id_type=MESH,
        )

    @pl.loop(1, NQ)
    def _(k):
        y_copy(k).start()

    core_copy(stage.at[y], stage.at[T_OTHER], 0).start()
    core_copy(z_ref, cbuf, 1).start()

    def row_copy(way, c):
        return pltpu.make_async_remote_copy(
            src_ref=rbuf.at[y, c],
            dst_ref=rbuf.at[y, c],
            send_sem=r_send.at[way, c],
            recv_sem=r_recv.at[way, c],
            device_id=(g, r, (y + 1 + 2 * way) % NQ),
            device_id_type=MESH,
        )

    def far_copy(way, c):
        q = (y + 3 + 2 * way) % NQ
        part = rbuf.at[q, c, pl.ds(pl.multiple_of(way * (SNP // 2), SNP // 2), SNP // 2)]
        return pltpu.make_async_remote_copy(
            src_ref=part,
            dst_ref=part,
            send_sem=f_send.at[way, c],
            recv_sem=f_recv.at[way, c],
            device_id=(g, r, (y + 1 + 2 * way) % NQ),
            device_id_type=MESH,
        )

    def send_chunk(step):
        row_copy(0, step).start()
        row_copy(1, step).start()

    def pass_on(step):
        for way in range(2):
            q = (y + 3 + 2 * way) % NQ
            pltpu.make_async_copy(
                rbuf.at[q, step], rbuf.at[q, step], r_recv.at[way, step]
            ).wait()
            far_copy(way, step).start()

    send_chunk(0)
    make_chunk(1)

    @pl.loop(1, NQ)
    def _(k):
        q = (y + k) % NQ
        pltpu.make_async_copy(stage.at[q], stage.at[q], y_recv.at[q]).wait()

    pltpu.make_async_copy(stage.at[T_OTHER], stage.at[T_OTHER], c_recv.at[0]).wait()

    def g_copy(k):
        return pltpu.make_async_remote_copy(
            src_ref=stage,
            dst_ref=allst.at[g],
            send_sem=g_send.at[k],
            recv_sem=g_recv.at[g],
            device_id=((g + k) % NB, r, y),
            device_id_type=MESH,
        )

    @pl.loop(1, NB)
    def _(k):
        g_copy(k).start()

    send_chunk(1)
    allst[g] = stage[...]
    make_chunk(2)
    make_chunk(3)
    pass_on(0)

    @pl.loop(1, NB)
    def _(k):
        b = (g + k) % NB
        pltpu.make_async_copy(allst.at[b], allst.at[b], g_recv.at[b]).wait()

    inv_b = []
    lds_b = []
    for b in range(NB):
        tile = allst[b, T_LD]
        inv_b.append(jnp.sum(jnp.sum(recip(tile), axis=0, keepdims=True), axis=1, keepdims=True))
        lds_b.append(jnp.sum(jnp.sum(tile, axis=0, keepdims=True), axis=1, keepdims=True))
    inv_t = functools.reduce(jnp.add, inv_b)
    lds_t = functools.reduce(jnp.add, lds_b)

    def slope(inv, ld, sums, count):
        return (inv * sums[4:8] - count * sums[0:4]) / (inv * ld - count * count)

    n_full = float(SNP * NB)
    n_del = float(SNP * (NB - 1))

    def total_of(q):
        total = allst[0, q]
        for b in range(1, NB):
            total = total + allst[b, q]
        return total

    def scaled(h):
        return lax.rsqrt(jnp.maximum(h, floor_value))

    for q in range(NQ):
        h = jnp.maximum(slope(inv_t, lds_t, total_of(q), n_full), 0.0)
        for c in range(NX):
            hpos[q * NX + c] = h[c : c + 1, :]
        for t in range(NT):
            hrow[q * NT + t] = jnp.concatenate(
                [h[c : c + 1, t * PART : (t + 1) * PART] for c in range(NX)], axis=1
            )

    for cb, q in ((r, y), (other, T_OTHER)):
        h_full = slope(inv_t, lds_t, total_of(q), n_full)
        hcols[cb, TROWS - 8 : TROWS, :] = jnp.zeros((8, TB), f32)
        for c in range(NX):
            lanes = slice(c * LANE, (c + 1) * LANE)
            hcols[cb, R_FULL : R_FULL + 1, lanes] = scaled(h_full[c : c + 1, :])
            hcols[cb, R_POS : R_POS + 1, lanes] = jnp.maximum(h_full[c : c + 1, :], 0.0)

    def weigh_columns(src, cb):
        @pl.loop(0, NCH)
        def _(s):
            rows = pl.ds(pl.multiple_of(s * LANE, LANE), LANE)
            for c in range(TB // LANE):
                lanes = slice(c * LANE, (c + 1) * LANE)
                h = hcols[cb, R_POS : R_POS + 1, lanes]
                u = recip(1.0 + h * ldcol[rows, :]).astype(bf16).astype(f32)
                colw[cb, rows, lanes] = (src[rows, lanes].astype(f32) * u).astype(bf16)

    weigh_columns(z_ref, r)
    pltpu.make_async_copy(cbuf, cbuf, c_recv.at[1]).wait()
    weigh_columns(cbuf, other)

    send_chunk(2)

    def part_rows(t):
        return pl.ds(pl.multiple_of(t * PART, PART), PART)

    def pair_copy(q, c, t):
        return pltpu.make_async_remote_copy(
            src_ref=sendy.at[q * NX + c, :, part_rows(t)],
            dst_ref=recvy.at[g, :, part_rows(t)],
            send_sem=a_send.at[q * NX + c, t],
            recv_sem=a_recv.at[g, t],
            device_id=(q * NX + c, r, y),
            device_id_type=MESH,
        )

    def extra_copy(c, t):
        return pltpu.make_async_remote_copy(
            src_ref=sendx.at[c, :, part_rows(t)],
            dst_ref=recvx.at[g, :, part_rows(t)],
            send_sem=e_send.at[c, t],
            recv_sem=e_recv.at[g, t],
            device_id=(y * NX + c, r, y),
            device_id_type=MESH,
        )

    def contract(left, right):
        return lax.dot_general(left, right, (((0,), (0,)), ((), ())), preferred_element_type=f32)

    def chunk_lanes(c):
        return pl.ds(pl.multiple_of((c % NX) * LANE, LANE), LANE)

    def half_lanes(side):
        return pl.ds(pl.multiple_of(side * HALF, HALF), HALF)

    def weigh_rows(q, t):
        h = hrow[q * NT + t]
        for s in range(NCH):
            rows = slice(s * LANE, (s + 1) * LANE)
            u = recip(1.0 + h * ldcol[rows, :]).astype(bf16).astype(f32)
            value = rbuf[q, t, rows, :].astype(f32) * u
            lhsy[rows, 0:LANE] = (value * lwcol[rows, :]).astype(bf16)
            lhsy[rows, LANE : 2 * LANE] = value.astype(bf16)

    def pair_sums(q, t):
        weigh_rows(q, t)
        cb = jnp.where(q > y, other, r)
        sums = contract(lhsy[...], colw[cb]).astype(bf16)
        for c in range(NX):
            for i in range(2):
                first = i * LANE + c * PART
                sendy[q * NX + c, i, part_rows(t), :] = sums[first : first + PART]

    def own_sums(t):
        weigh_rows(y, t)
        own = contract(lhsy[...], colw[r]).astype(bf16)
        cross = contract(lhsy[...], colw[other])
        low, high = cross[:, 0:HALF], cross[:, HALF:TB]
        sides = (
            jnp.where(r == 0, low, high).astype(bf16),
            jnp.where(r == 0, high, low).astype(bf16),
        )
        for c in range(NX):
            near, after = (c + 1) % NX * LANE, (c + 2) % NX * LANE
            for i in range(2):
                rows = slice(i * LANE + c * PART, i * LANE + (c + 1) * PART)
                dst = y * NX + c
                sendy[dst, i, part_rows(t), 0:HALF] = sides[c // 2][rows]
                sendy[dst, i, part_rows(t), HALF : HALF + LANE] = own[
                    rows, c * LANE : (c + 1) * LANE
                ]
                sendy[dst, i, part_rows(t), HALF + LANE : TB] = own[rows, near : near + LANE]
                if c < 2:
                    sendx[c, i, part_rows(t), :] = own[rows, after : after + LANE]

    def deliver(t):
        for dz, dx in ORDER:
            pair_copy((zz + dz) % NQ, (x + dx) % NX, t).start()

        recvy[g, :, part_rows(t), :] = sendy[g, :, part_rows(t), :]

        @pl.loop(0, 2)
        def _(c):
            @pl.when(y * NX + c == g)
            def _():
                recvx[g, :, part_rows(t), :] = sendx[c, :, part_rows(t), :]

            @pl.when(y * NX + c != g)
            def _():
                extra_copy(c, t).start()

    def make_table(rows):
        @pl.when(jnp.logical_not(diag))
        def _():
            ctab[rows, 0:TB] = hcols[own_cb, rows, :]
            ctab[rows, TB : TB + LANE] = hcols[own_cb, rows, 0:LANE]

        @pl.when(diag)
        def _():
            ctab[rows, 0:HALF] = hcols[other, rows, half_lanes(half)]
            for i in range(3):
                ctab[rows, HALF + i * LANE : HALF + (i + 1) * LANE] = hcols[
                    r, rows, chunk_lanes(x + i)
                ]

    make_table(slice(TROWS - 8, TROWS))
    hdr[...] = jnp.zeros((LANE, LANE), f32)
    hdr[R_POS : R_POS + 1, :] = hpos[zz * NX + x]
    hdt[...] = jnp.transpose(hdr[...])

    def weight_sums(b):
        tile = allst[b, T_LD]
        inv = recip(tile)
        h = hdt[:, R_POS : R_POS + 1]
        for c in range(NCH):
            lanes = slice(c * LANE, (c + 1) * LANE)
            row = tile[c : c + 1, :]
            u16 = recip(1.0 + h * row).astype(bf16)
            u = u16.astype(f32)
            lhsw[0:ROWS, lanes] = (u * inv[c : c + 1, :]).astype(bf16)
            lhsw[ROWS : 2 * ROWS, lanes] = u16
            lhsw[2 * ROWS : 3 * ROWS, lanes] = (u * row).astype(bf16)
        ldc = column_tile(tile)
        h = ctab[R_POS : R_POS + 1, 0:TB]
        for c in range(NCH):
            ucol[c * LANE : (c + 1) * LANE, :] = recip(1.0 + ldc[:, c : c + 1] * h).astype(bf16)
        wbuf[b] = jnp.dot(lhsw[...], ucol[...], preferred_element_type=f32)

        @pl.when(fifth)
        def _():
            h = ctab[R_POS : R_POS + 1, TB : TB + LANE]
            for c in range(NCH):
                ucol[c * LANE : (c + 1) * LANE, 0:LANE] = recip(1.0 + ldc[:, c : c + 1] * h).astype(
                    bf16
                )
            wext[b] = jnp.dot(lhsw[...], ucol[:, 0:LANE], preferred_element_type=f32)

    @pl.loop(0, NX)
    def _(step):
        far = (y + 2) % NQ
        for way in range(2):
            part = rbuf.at[far, step, pl.ds(way * (SNP // 2), SNP // 2)]
            pltpu.make_async_copy(part, part, f_recv.at[way, step]).wait()

        @pl.loop(0, NQ)
        def _(k):
            @pl.when(k == y)
            def _():
                own_sums(step)

            @pl.when(k != y)
            def _():
                pair_sums(k, step)

        deliver(step)

        @pl.when(step < NT - 1)
        def _():
            pass_on(step + 1)

        @pl.loop(0, W_STEP)
        def _(k):
            weight_sums(step * W_STEP + k)

        @pl.when(step == 0)
        def _():
            send_chunk(NT - 1)

    @pl.loop(NT * W_STEP, NB)
    def _(b):
        weight_sums(b)

    for cb, q in ((r, y), (other, T_OTHER)):
        total = total_of(q)
        for b in range(NB):
            h = scaled(slope(inv_t - inv_b[b], lds_t - lds_b[b], total - allst[b, q], n_del))
            for c in range(NX):
                hcols[cb, b : b + 1, c * LANE : (c + 1) * LANE] = h[c : c + 1, :]
    make_table(slice(0, NB))
    total = total_of(zz)
    h_full = scaled(slope(inv_t, lds_t, total, n_full))
    for c in range(NX):
        hdq[R_FULL, c] = h_full[c : c + 1, :]
    for b in range(NB):
        h = scaled(slope(inv_t - inv_b[b], lds_t - lds_b[b], total - allst[b, zz], n_del))
        for c in range(NX):
            hdq[b, c] = h[c : c + 1, :]
    for b in range(NB + 1):
        hdr[b : b + 1, :] = hdq[b, x]
    hdt[...] = jnp.transpose(hdr[...])

    def factors(weights, full, first, width):
        @pl.loop(0, ROWS // 8)
        def _(t):
            base = pl.multiple_of(t * 8, 8)

            def at(i):
                return pl.ds(i * ROWS + base, 8)

            for c in range(width // LANE):
                lanes = slice(c * LANE, (c + 1) * LANE)
                tlanes = slice(first + c * LANE, first + (c + 1) * LANE)
                tot = [weights[0, at(i), lanes] for i in range(3)]
                for b in range(1, NB):
                    tot = [tot[i] + weights[b, at(i), lanes] for i in range(3)]

                def pair(w, b):
                    scale = hdt[pl.ds(base, 8), b : b + 1] * ctab[b : b + 1, tlanes]
                    k = scale / (w[0] * w[2] - w[1] * w[1])
                    return w[0] * k, w[1] * k

                full[0, pl.ds(base, 8), lanes], full[1, pl.ds(base, 8), lanes] = pair(tot, R_FULL)
                for b in range(NB):
                    w = [tot[i] - weights[b, at(i), lanes] for i in range(3)]
                    weights[b, at(0), lanes], weights[b, at(1), lanes] = pair(w, b)

    factors(wbuf, wfull, 0, TB)

    @pl.when(fifth)
    def _():
        factors(wext, wfext, TB, LANE)

    def place(j):
        on_half = j < 2
        cb = jnp.where(jnp.logical_not(diag), own_cb, jnp.where(on_half, other, r))
        chunk = jnp.where(
            jnp.logical_not(diag), j, jnp.where(on_half, 2 * half + j, (x + j + 2) % NX)
        )
        return cb, chunk

    def mirror_copy(j, t):
        cb, chunk = place(j)
        slot = jnp.where(jnp.logical_and(diag, j >= 2), j + 1, x)
        return pltpu.make_async_remote_copy(
            src_ref=msend.at[j, :, part_rows(t)],
            dst_ref=mrecv.at[slot, :, part_rows(t)],
            send_sem=m_send.at[j, t],
            recv_sem=m_recv.at[slot, t],
            device_id=(y * NX + chunk, cb, zz),
            device_id_type=MESH,
        )

    def sends(j):
        return jnp.logical_not(jnp.logical_and(diag, j == 2))

    def finish(pairs, weights, full, j, first, t):
        cb, chunk = place(j)
        out = chunk_lanes(chunk)
        lanes = pl.ds(pl.multiple_of(first, LANE), LANE)

        @pl.loop(0, PART // 16)
        def _(i):
            base = pl.multiple_of(t * PART + i * 16, 16)
            rows = pl.ds(base, 16)
            tot0 = pairs[0, 0, rows, lanes].astype(f32)
            tot1 = pairs[0, 1, rows, lanes].astype(f32)
            for b in range(1, NB):
                tot0 = tot0 + pairs[b, 0, rows, lanes].astype(f32)
                tot1 = tot1 + pairs[b, 1, rows, lanes].astype(f32)
            rg = full[0, rows, lanes] * tot1 - full[1, rows, lanes] * tot0
            rg_ref[cb, rows, out] = rg
            msend[j, 0, rows, :] = rg.astype(bf16)
            values = []
            for b in range(NB):
                del0 = tot0 - pairs[b, 0, rows, lanes].astype(f32)
                del1 = tot1 - pairs[b, 1, rows, lanes].astype(f32)
                values.append(
                    weights[b, pl.ds(base, 16), lanes] * del1
                    - weights[b, pl.ds(ROWS + base, 16), lanes] * del0
                )
            mean = functools.reduce(jnp.add, values) * (1.0 / NB)
            spread = functools.reduce(jnp.add, [(v - mean) * (v - mean) for v in values])
            se = jnp.sqrt((NB - 1) / NB * spread)
            se_ref[cb, rows, out] = se
            msend[j, 1, rows, :] = se.astype(bf16)

        @pl.when(sends(j))
        def _():
            mirror_copy(j, t).start()

    @pl.loop(0, NT)
    def _(t):
        @pl.loop(1, NB)
        def _(k):
            part = recvy.at[(g + k) % NB, :, part_rows(t)]
            pltpu.make_async_copy(part, part, a_recv.at[(g + k) % NB, t]).wait()

        @pl.loop(0, NX)
        def _(j):
            finish(recvy, wbuf, wfull, j, j * LANE, t)

        @pl.when(fifth)
        def _():
            @pl.loop(1, NB)
            def _(k):
                part = recvx.at[(g + k) % NB, :, part_rows(t)]
                pltpu.make_async_copy(part, part, e_recv.at[(g + k) % NB, t]).wait()

            finish(recvx, wext, wfext, NX, 0, t)

    def take(slot, cb, chunk):
        @pl.loop(0, NT)
        def _(t):
            part = mrecv.at[slot, :, part_rows(t)]
            pltpu.make_async_copy(part, part, m_recv.at[slot, t]).wait()

        lanes = chunk_lanes(chunk)
        rg_ref[cb, :, lanes] = jnp.transpose(mrecv[slot, 0].astype(f32))
        se_ref[cb, :, lanes] = jnp.transpose(mrecv[slot, 1].astype(f32))

    @pl.when(jnp.logical_not(diag))
    def _():
        @pl.loop(0, NX)
        def _(k):
            take(k, 1 - own_cb, k)

    @pl.when(diag)
    def _():
        @pl.loop(0, 2)
        def _(k):
            chunk = 2 * (1 - half) + k
            take(chunk, other, chunk)

        take(NX, r, x + 3)

        @pl.when(x >= 2)
        def _():
            take(NX + 1, r, x + 2)

    @pl.loop(1, NQ)
    def _(k):
        y_copy(k).wait_send()

    core_copy(stage.at[y], stage.at[T_OTHER], 0).wait_send()
    core_copy(z_ref, cbuf, 1).wait_send()

    @pl.loop(0, NX)
    def _(c):
        for way in range(2):
            row_copy(way, c).wait_send()
            far_copy(way, c).wait_send()

    @pl.loop(1, NB)
    def _(k):
        g_copy(k).wait_send()
        p = (g + k) % NB

        @pl.loop(0, NT)
        def _(t):
            pair_copy(p // NX, p % NX, t).wait_send()

    @pl.loop(0, NT)
    def _(t):
        @pl.loop(0, 2)
        def _(c):
            @pl.when(y * NX + c != g)
            def _():
                extra_copy(c, t).wait_send()

        @pl.loop(0, NX)
        def _(j):
            @pl.when(sends(j))
            def _():
                mirror_copy(j, t).wait_send()

        @pl.when(fifth)
        def _():
            mirror_copy(NX, t).wait_send()


def per_device(ldscore, zscores):
    dma = pltpu.SemaphoreType.DMA
    out = jax.ShapeDtypeStruct((2, ROWS, TB), f32)
    rg, se = pl.pallas_call(
        kernel,
        out_shape=(out, out),
        in_specs=[pl.BlockSpec(memory_space=pltpu.VMEM)] * 2,
        out_specs=[pl.BlockSpec(memory_space=pltpu.VMEM)] * 2,
        scratch_shapes=[
            pltpu.VMEM((T_LD + 1, 8, LANE), f32),
            pltpu.VMEM((NB, T_LD + 1, 8, LANE), f32),
            pltpu.VMEM((SNP, LANE), f32),
            pltpu.VMEM((SNP, LANE), f32),
            pltpu.VMEM((NQ * NT, 1, LANE), f32),
            pltpu.VMEM((NQ * NX, 1, LANE), f32),
            pltpu.VMEM((R_POS + 1, NX, 1, LANE), f32),
            pltpu.VMEM((LANE, LANE), f32),
            pltpu.VMEM((LANE, LANE), f32),
            pltpu.VMEM((2, TROWS, TB), f32),
            pltpu.VMEM((TROWS, TB + LANE), f32),
            pltpu.VMEM((NQ, NT, SNP, LANE), bf16),
            pltpu.VMEM((SNP, TB), bf16),
            pltpu.VMEM((2, SNP, TB), bf16),
            pltpu.VMEM((SNP, 2 * LANE), bf16),
            pltpu.VMEM((NB, 2, ROWS, TB), bf16),
            pltpu.VMEM((2, 2, ROWS, LANE), bf16),
            pltpu.VMEM((NB, 2, ROWS, TB), bf16),
            pltpu.VMEM((NB, 2, ROWS, LANE), bf16),
            pltpu.VMEM((3 * ROWS, SNP), bf16),
            pltpu.VMEM((SNP, TB), bf16),
            pltpu.VMEM((NB, 3 * ROWS, TB), f32),
            pltpu.VMEM((NB, 3 * ROWS, LANE), f32),
            pltpu.VMEM((2, ROWS, TB), f32),
            pltpu.VMEM((2, ROWS, LANE), f32),
            pltpu.VMEM((NX + 1, 2, LANE, LANE), bf16),
            pltpu.VMEM((NX + 2, 2, LANE, LANE), bf16),
            dma((NQ,)),
            dma((NQ,)),
            dma((NB,)),
            dma((NB,)),
            dma((2,)),
            dma((2,)),
            dma((2, NT)),
            dma((2, NT)),
            dma((2, NT)),
            dma((2, NT)),
            dma((NB, NT)),
            dma((NB, NT)),
            dma((2, NT)),
            dma((NB, NT)),
            dma((NX + 1, NT)),
            dma((NX + 2, NT)),
        ],
        compiler_params=pltpu.CompilerParams(
            collective_id=0, has_side_effects=True, vmem_limit_bytes=56 * 1024 * 1024
        ),
    )(ldscore.reshape(8, LANE), zscores)
    return (rg.transpose(1, 0, 2)[None], se.transpose(1, 0, 2)[None])


def solution(mesh):
    return jax.shard_map(
        per_device,
        mesh=mesh,
        in_specs=(P("genome"), P("genome", ("trow", "tcol"))),
        out_specs=(P("trow", "genome", None, "tcol"), P("trow", "genome", None, "tcol")),
        check_vma=False,
    )
```

```python
import functools

import jax
import jax.numpy as jnp
from jax import lax
from jax.experimental import pallas as pl
from jax.experimental.pallas import tpu as pltpu
from jax.sharding import PartitionSpec as P

floor_value = 0.002
MESH = pl.DeviceIdType.MESH
f32 = jnp.float32
bf16 = jnp.bfloat16

SNP = 1024
TB = 512
LANE = 128
NCH = SNP // LANE
NB = 16
NQ = 4
NX = 4
ROWS = 128

R_FULL = NB
R_POS = NB + 1
TROWS = 24

T_OTHER = NQ
T_LD = NQ + 1

W_STEP = 4

NT = 4
PART = ROWS // NT
ORDER = (
    (2, 2), (1, 1), (3, 3), (1, 3), (3, 1), (1, 2), (3, 2), (2, 1), (2, 3),
    (0, 1), (1, 0), (0, 3), (3, 0), (0, 2), (2, 0),
)

DIAG = (
    ((3, 4, 5, 6), (1, 2, 5, 6, 7), (0, 1, 6, 7, 2), (0, 1, 7, 4)),
    ((0, 1, 4, 5, 6), (0, 5, 6, 7), (0, 3, 6, 7), (1, 2, 7, 4, 3)),
)


def digits(chunks):
    return sum(d << (4 * i) for i, d in enumerate(chunks))


def recip(value):
    return 1.0 / value


def column_tile(tile):
    return jnp.transpose(jnp.concatenate([tile] * (LANE // 8), axis=0))


def kernel(
    ld_ref,
    z_ref,
    rg_ref,
    se_ref,
    stage,
    allst,
    ldcol,
    lwcol,
    hrow,
    hpos,
    hdq,
    hdr,
    hdt,
    hcols,
    ctab,
    rbuf,
    cbuf,
    colw,
    lhsy,
    sendy,
    sendx,
    recvy,
    recvx,
    lhsw,
    ucol,
    wbuf,
    wext,
    fbuf,
    fext,
    wfull,
    wfext,
    msend,
    mrecv,
    y_send,
    y_recv,
    g_send,
    g_recv,
    c_send,
    c_recv,
    r_send,
    r_recv,
    f_send,
    f_recv,
    a_send,
    a_recv,
    e_send,
    e_recv,
    m_send,
    m_recv,
):
    g = lax.axis_index("genome")
    r = lax.axis_index("trow")
    y = lax.axis_index("tcol")
    zz = g // NX
    x = g % NX
    other = 1 - r
    diag = zz == y
    own_cb = jnp.where(zz > y, other, r)
    code = jnp.int32(0)
    for core in range(2):
        for at_x in range(NX):
            here = jnp.logical_and(r == core, x == at_x)
            code = jnp.where(here, digits(DIAG[core][at_x]), code)
    fifth = jnp.logical_and(diag, ((x + 1) // 2 + r) % 2 == 1)

    barrier = pltpu.get_barrier_semaphore()

    def greet(dev):
        pl.semaphore_signal(barrier, inc=1, device_id=dev, device_id_type=MESH)

    @pl.loop(1, NB)
    def _(k):
        greet(((g + k) % NB, r, y))

    @pl.loop(1, NQ)
    def _(k):
        greet((g, r, (y + k) % NQ))

    greet((g, other, y))

    @pl.when(diag)
    def _():
        @pl.loop(0, NX)
        def _(k):
            greet((zz * NX + k, other, y))

    @pl.when(jnp.logical_not(diag))
    def _():
        @pl.loop(0, NX)
        def _(k):
            greet((y * NX + k, r, zz))
            greet((y * NX + k, other, zz))

    ld_tile = ld_ref[...]
    ld_t = column_tile(ld_tile)
    for c in range(NCH):
        col = jnp.broadcast_to(ld_t[:, c : c + 1], (LANE, LANE))
        ldcol[c * LANE : (c + 1) * LANE, :] = col
        lwcol[c * LANE : (c + 1) * LANE, :] = recip(col)
    for c in range(TB // LANE):
        lanes = slice(c * LANE, (c + 1) * LANE)
        acc_y = jnp.zeros((8, LANE), f32)
        acc_l = jnp.zeros((8, LANE), f32)
        for s in range(NCH):
            rows = slice(s * LANE, (s + 1) * LANE)
            zc = z_ref[rows, lanes].astype(f32)
            sq = zc * zc
            acc_l = acc_l + jnp.sum(sq.reshape(LANE // 8, 8, LANE), axis=0)
            acc_y = acc_y + jnp.sum((sq * lwcol[rows, :]).reshape(LANE // 8, 8, LANE), axis=0)
        stage[y, c : c + 1, :] = jnp.sum(acc_y, axis=0, keepdims=True)
        stage[y, 4 + c : 5 + c, :] = jnp.sum(acc_l, axis=0, keepdims=True)
    stage[T_LD] = ld_tile

    def gather_parts(value, t):
        return jnp.concatenate(
            [value[:, c * LANE + t * PART : c * LANE + (t + 1) * PART] for c in range(NX)], axis=1
        )

    def make_chunk(t):
        for s in range(NCH):
            rows = slice(s * LANE, (s + 1) * LANE)
            rbuf[y, t, rows, :] = gather_parts(z_ref[rows, :], t)

    make_chunk(0)

    @pl.when(diag)
    def _():
        pl.semaphore_wait(barrier, NB - 1 + NQ - 1 + 1 + NX)

    @pl.when(jnp.logical_not(diag))
    def _():
        pl.semaphore_wait(barrier, NB - 1 + NQ - 1 + 1 + 2 * NX)

    def y_copy(k):
        return pltpu.make_async_remote_copy(
            src_ref=stage.at[y],
            dst_ref=stage.at[y],
            send_sem=y_send.at[k],
            recv_sem=y_recv.at[y],
            device_id=(g, r, (y + k) % NQ),
            device_id_type=MESH,
        )

    def core_copy(src, dst, i):
        return pltpu.make_async_remote_copy(
            src_ref=src,
            dst_ref=dst,
            send_sem=c_send.at[i],
            recv_sem=c_recv.at[i],
            device_id=(g, other, y),
            device_id_type=MESH,
        )

    @pl.loop(1, NQ)
    def _(k):
        y_copy(k).start()

    core_copy(stage.at[y], stage.at[T_OTHER], 0).start()
    core_copy(z_ref, cbuf, 1).start()

    def row_copy(way, c):
        return pltpu.make_async_remote_copy(
            src_ref=rbuf.at[y, c],
            dst_ref=rbuf.at[y, c],
            send_sem=r_send.at[way, c],
            recv_sem=r_recv.at[way, c],
            device_id=(g, r, (y + 1 + 2 * way) % NQ),
            device_id_type=MESH,
        )

    def far_copy(way, c):
        q = (y + 3 + 2 * way) % NQ
        part = rbuf.at[q, c, pl.ds(pl.multiple_of(way * (SNP // 2), SNP // 2), SNP // 2)]
        return pltpu.make_async_remote_copy(
            src_ref=part,
            dst_ref=part,
            send_sem=f_send.at[way, c],
            recv_sem=f_recv.at[way, c],
            device_id=(g, r, (y + 1 + 2 * way) % NQ),
            device_id_type=MESH,
        )

    def send_chunk(step):
        row_copy(0, step).start()
        row_copy(1, step).start()

    def pass_on(step):
        for way in range(2):
            q = (y + 3 + 2 * way) % NQ
            pltpu.make_async_copy(
                rbuf.at[q, step], rbuf.at[q, step], r_recv.at[way, step]
            ).wait()
            far_copy(way, step).start()

    send_chunk(0)
    make_chunk(1)

    @pl.loop(1, NQ)
    def _(k):
        q = (y + k) % NQ
        pltpu.make_async_copy(stage.at[q], stage.at[q], y_recv.at[q]).wait()

    pltpu.make_async_copy(stage.at[T_OTHER], stage.at[T_OTHER], c_recv.at[0]).wait()

    def g_copy(k):
        return pltpu.make_async_remote_copy(
            src_ref=stage,
            dst_ref=allst.at[g],
            send_sem=g_send.at[k],
            recv_sem=g_recv.at[g],
            device_id=((g + k) % NB, r, y),
            device_id_type=MESH,
        )

    @pl.loop(1, NB)
    def _(k):
        g_copy(k).start()

    send_chunk(1)
    allst[g] = stage[...]
    make_chunk(2)
    make_chunk(3)
    pass_on(0)

    @pl.loop(1, NB)
    def _(k):
        b = (g + k) % NB
        pltpu.make_async_copy(allst.at[b], allst.at[b], g_recv.at[b]).wait()

    inv_b = []
    lds_b = []
    for b in range(NB):
        tile = allst[b, T_LD]
        inv_b.append(jnp.sum(jnp.sum(recip(tile), axis=0, keepdims=True), axis=1, keepdims=True))
        lds_b.append(jnp.sum(jnp.sum(tile, axis=0, keepdims=True), axis=1, keepdims=True))
    inv_t = functools.reduce(jnp.add, inv_b)
    lds_t = functools.reduce(jnp.add, lds_b)

    def slope(inv, ld, sums, count):
        return (inv * sums[4:8] - count * sums[0:4]) / (inv * ld - count * count)

    n_full = float(SNP * NB)
    n_del = float(SNP * (NB - 1))

    def total_of(q):
        total = allst[0, q]
        for b in range(1, NB):
            total = total + allst[b, q]
        return total

    def scaled(h):
        return lax.rsqrt(jnp.maximum(h, floor_value))

    for q in range(NQ):
        h = jnp.maximum(slope(inv_t, lds_t, total_of(q), n_full), 0.0)
        for c in range(NX):
            hpos[q * NX + c] = h[c : c + 1, :]
        for t in range(NT):
            hrow[q * NT + t] = jnp.concatenate(
                [h[c : c + 1, t * PART : (t + 1) * PART] for c in range(NX)], axis=1
            )

    for cb, q in ((r, y), (other, T_OTHER)):
        h_full = slope(inv_t, lds_t, total_of(q), n_full)
        hcols[cb, TROWS - 8 : TROWS, :] = jnp.zeros((8, TB), f32)
        for c in range(NX):
            lanes = slice(c * LANE, (c + 1) * LANE)
            hcols[cb, R_FULL : R_FULL + 1, lanes] = scaled(h_full[c : c + 1, :])
            hcols[cb, R_POS : R_POS + 1, lanes] = jnp.maximum(h_full[c : c + 1, :], 0.0)

    def weigh_columns(src, cb):
        @pl.loop(0, NCH)
        def _(s):
            rows = pl.ds(pl.multiple_of(s * LANE, LANE), LANE)
            for c in range(TB // LANE):
                lanes = slice(c * LANE, (c + 1) * LANE)
                h = hcols[cb, R_POS : R_POS + 1, lanes]
                u = recip(1.0 + h * ldcol[rows, :]).astype(bf16).astype(f32)
                colw[cb, rows, lanes] = (src[rows, lanes].astype(f32) * u).astype(bf16)

    weigh_columns(z_ref, r)
    pltpu.make_async_copy(cbuf, cbuf, c_recv.at[1]).wait()
    weigh_columns(cbuf, other)

    send_chunk(2)

    def part_rows(t):
        return pl.ds(pl.multiple_of(t * PART, PART), PART)

    def pair_copy(q, c, t):
        return pltpu.make_async_remote_copy(
            src_ref=sendy.at[q * NX + c, :, part_rows(t)],
            dst_ref=recvy.at[g, :, part_rows(t)],
            send_sem=a_send.at[q * NX + c, t],
            recv_sem=a_recv.at[g, t],
            device_id=(q * NX + c, r, y),
            device_id_type=MESH,
        )

    def fifth_x(e):
        return jnp.where(r == 0, 1 + e, 3 * e)

    def extra_copy(e, t):
        return pltpu.make_async_remote_copy(
            src_ref=sendx.at[e, :, part_rows(t)],
            dst_ref=recvx.at[g, :, part_rows(t)],
            send_sem=e_send.at[e, t],
            recv_sem=e_recv.at[g, t],
            device_id=(y * NX + fifth_x(e), r, y),
            device_id_type=MESH,
        )

    def contract(left, right):
        return lax.dot_general(left, right, (((0,), (0,)), ((), ())), preferred_element_type=f32)

    def chunk_lanes(c):
        return pl.ds(pl.multiple_of((c % NX) * LANE, LANE), LANE)

    def weigh_rows(q, t):
        h = hrow[q * NT + t]
        for s in range(NCH):
            rows = slice(s * LANE, (s + 1) * LANE)
            u = recip(1.0 + h * ldcol[rows, :]).astype(bf16).astype(f32)
            value = rbuf[q, t, rows, :].astype(f32) * u
            lhsy[rows, 0:LANE] = (value * lwcol[rows, :]).astype(bf16)
            lhsy[rows, LANE : 2 * LANE] = value.astype(bf16)

    def pair_sums(q, t):
        weigh_rows(q, t)
        cb = jnp.where(q > y, other, r)
        sums = contract(lhsy[...], colw[cb]).astype(bf16)
        for c in range(NX):
            for i in range(2):
                first = i * LANE + c * PART
                sendy[q * NX + c, i, part_rows(t), :] = sums[first : first + PART]

    def own_sums(t):
        weigh_rows(y, t)
        sums = (
            contract(lhsy[...], colw[other]).astype(bf16),
            contract(lhsy[...], colw[r]).astype(bf16),
        )

        def piece(core, c, k, i):
            d = DIAG[core][c][k]
            rows = slice(i * LANE + c * PART, i * LANE + (c + 1) * PART)
            return sums[d // NX][rows, d % NX * LANE : (d % NX + 1) * LANE]

        def pick(zero, one):
            return jnp.where(r == 0, zero.astype(f32), one.astype(f32)).astype(bf16)

        for i in range(2):
            for c in range(NX):
                for k in range(4):
                    sendy[y * NX + c, i, part_rows(t), k * LANE : (k + 1) * LANE] = pick(
                        piece(0, c, k, i), piece(1, c, k, i)
                    )
            for e in range(2):
                sendx[e, i, part_rows(t), :] = pick(piece(0, 1 + e, 4, i), piece(1, 3 * e, 4, i))

    def deliver(t):
        for dz, dx in ORDER:
            pair_copy((zz + dz) % NQ, (x + dx) % NX, t).start()

        recvy[g, :, part_rows(t), :] = sendy[g, :, part_rows(t), :]

        @pl.loop(0, 2)
        def _(e):
            @pl.when(y * NX + fifth_x(e) == g)
            def _():
                recvx[g, :, part_rows(t), :] = sendx[e, :, part_rows(t), :]

            @pl.when(y * NX + fifth_x(e) != g)
            def _():
                extra_copy(e, t).start()

    def place(j):
        d = (code >> (4 * j)) & 7
        cb = jnp.where(diag, jnp.where(d >= NX, r, other), own_cb)
        return cb, jnp.where(diag, d % NX, j % NX)

    def make_table(rows):
        for k in range(NX + 1):
            cb, chunk = place(k)
            ctab[rows, k * LANE : (k + 1) * LANE] = hcols[cb, rows, chunk_lanes(chunk)]

    make_table(slice(TROWS - 8, TROWS))
    hdr[...] = jnp.zeros((LANE, LANE), f32)
    hdr[R_POS : R_POS + 1, :] = hpos[zz * NX + x]
    hdt[...] = jnp.transpose(hdr[...])

    def weight_sums(b):
        tile = allst[b, T_LD]
        inv = recip(tile)
        h = hdt[:, R_POS : R_POS + 1]
        for c in range(NCH):
            lanes = slice(c * LANE, (c + 1) * LANE)
            row = tile[c : c + 1, :]
            u16 = recip(1.0 + h * row).astype(bf16)
            u = u16.astype(f32)
            lhsw[0:ROWS, lanes] = (u * inv[c : c + 1, :]).astype(bf16)
            lhsw[ROWS : 2 * ROWS, lanes] = u16
            lhsw[2 * ROWS : 3 * ROWS, lanes] = (u * row).astype(bf16)
        ldc = column_tile(tile)
        h = ctab[R_POS : R_POS + 1, 0:TB]
        for c in range(NCH):
            ucol[c * LANE : (c + 1) * LANE, :] = recip(1.0 + ldc[:, c : c + 1] * h).astype(bf16)
        wbuf[b] = jnp.dot(lhsw[...], ucol[...], preferred_element_type=f32)

        @pl.when(fifth)
        def _():
            h = ctab[R_POS : R_POS + 1, TB : TB + LANE]
            for c in range(NCH):
                ucol[c * LANE : (c + 1) * LANE, 0:LANE] = recip(1.0 + ldc[:, c : c + 1] * h).astype(
                    bf16
                )
            wext[b] = jnp.dot(lhsw[...], ucol[:, 0:LANE], preferred_element_type=f32)

    @pl.loop(0, NX)
    def _(step):
        far = (y + 2) % NQ
        for way in range(2):
            part = rbuf.at[far, step, pl.ds(way * (SNP // 2), SNP // 2)]
            pltpu.make_async_copy(part, part, f_recv.at[way, step]).wait()

        @pl.loop(0, NQ)
        def _(k):
            @pl.when(k == y)
            def _():
                own_sums(step)

            @pl.when(k != y)
            def _():
                pair_sums(k, step)

        deliver(step)

        @pl.when(step < NT - 1)
        def _():
            pass_on(step + 1)

        @pl.loop(0, W_STEP)
        def _(k):
            weight_sums(step * W_STEP + k)

        @pl.when(step == 0)
        def _():
            send_chunk(NT - 1)

    @pl.loop(NT * W_STEP, NB)
    def _(b):
        weight_sums(b)

    for cb, q in ((r, y), (other, T_OTHER)):
        total = total_of(q)
        for b in range(NB):
            h = scaled(slope(inv_t - inv_b[b], lds_t - lds_b[b], total - allst[b, q], n_del))
            for c in range(NX):
                hcols[cb, b : b + 1, c * LANE : (c + 1) * LANE] = h[c : c + 1, :]
    make_table(slice(0, NB))
    total = total_of(zz)
    h_full = scaled(slope(inv_t, lds_t, total, n_full))
    for c in range(NX):
        hdq[R_FULL, c] = h_full[c : c + 1, :]
    for b in range(NB):
        h = scaled(slope(inv_t - inv_b[b], lds_t - lds_b[b], total - allst[b, zz], n_del))
        for c in range(NX):
            hdq[b, c] = h[c : c + 1, :]
    for b in range(NB + 1):
        hdr[b : b + 1, :] = hdq[b, x]
    hdt[...] = jnp.transpose(hdr[...])

    def factors(weights, parts, full, first, width):
        @pl.loop(0, ROWS // 8)
        def _(t):
            base = pl.multiple_of(t * 8, 8)

            def at(i):
                return pl.ds(i * ROWS + base, 8)

            for c in range(width // LANE):
                lanes = slice(c * LANE, (c + 1) * LANE)
                tlanes = slice(first + c * LANE, first + (c + 1) * LANE)
                tot = [weights[0, at(i), lanes] for i in range(3)]
                for b in range(1, NB):
                    tot = [tot[i] + weights[b, at(i), lanes] for i in range(3)]

                def pair(w, b):
                    scale = hdt[pl.ds(base, 8), b : b + 1] * ctab[b : b + 1, tlanes]
                    k = scale / (w[0] * w[2] - w[1] * w[1])
                    return w[0] * k, w[1] * k

                full[0, pl.ds(base, 8), lanes], full[1, pl.ds(base, 8), lanes] = pair(tot, R_FULL)
                for b in range(NB):
                    w = [tot[i] - weights[b, at(i), lanes] for i in range(3)]
                    parts[b, at(0), lanes], parts[b, at(1), lanes] = pair(w, b)

    factors(wbuf, fbuf, wfull, 0, TB)

    @pl.when(fifth)
    def _():
        factors(wext, fext, wfext, TB, LANE)

    def mirror_copy(j, t):
        cb, chunk = place(j)
        slot = jnp.where(jnp.logical_and(diag, cb == r), NX + x, x)
        return pltpu.make_async_remote_copy(
            src_ref=msend.at[j, :, part_rows(t)],
            dst_ref=mrecv.at[slot, :, part_rows(t)],
            send_sem=m_send.at[j, t],
            recv_sem=m_recv.at[slot, t],
            device_id=(y * NX + chunk, cb, zz),
            device_id_type=MESH,
        )

    def sends(j):
        cb, chunk = place(j)
        return jnp.logical_not(diag & (cb == r) & (chunk == x))

    def finish(pairs, weights, full, j, first, t):
        cb, chunk = place(j)
        out = chunk_lanes(chunk)
        lanes = pl.ds(pl.multiple_of(first, LANE), LANE)

        @pl.loop(0, PART // 16)
        def _(i):
            base = pl.multiple_of(t * PART + i * 16, 16)
            rows = pl.ds(base, 16)
            tot0 = pairs[0, 0, rows, lanes].astype(f32)
            tot1 = pairs[0, 1, rows, lanes].astype(f32)
            for b in range(1, NB):
                tot0 = tot0 + pairs[b, 0, rows, lanes].astype(f32)
                tot1 = tot1 + pairs[b, 1, rows, lanes].astype(f32)
            rg = full[0, rows, lanes] * tot1 - full[1, rows, lanes] * tot0
            rg_ref[cb, rows, out] = rg
            msend[j, 0, rows, :] = rg.astype(bf16)
            values = []
            for b in range(NB):
                del0 = tot0 - pairs[b, 0, rows, lanes].astype(f32)
                del1 = tot1 - pairs[b, 1, rows, lanes].astype(f32)
                values.append(
                    weights[b, pl.ds(base, 16), lanes] * del1
                    - weights[b, pl.ds(ROWS + base, 16), lanes] * del0
                )
            mean = functools.reduce(jnp.add, values) * (1.0 / NB)
            spread = functools.reduce(jnp.add, [(v - mean) * (v - mean) for v in values])
            se = jnp.sqrt((NB - 1) / NB * spread)
            se_ref[cb, rows, out] = se
            msend[j, 1, rows, :] = se.astype(bf16)

        @pl.when(sends(j))
        def _():
            mirror_copy(j, t).start()

    @pl.loop(0, NT)
    def _(t):
        @pl.loop(1, NB)
        def _(k):
            part = recvy.at[(g + k) % NB, :, part_rows(t)]
            pltpu.make_async_copy(part, part, a_recv.at[(g + k) % NB, t]).wait()

        @pl.loop(0, NX)
        def _(j):
            finish(recvy, fbuf, wfull, j, j * LANE, t)

        @pl.when(fifth)
        def _():
            @pl.loop(1, NB)
            def _(k):
                part = recvx.at[(g + k) % NB, :, part_rows(t)]
                pltpu.make_async_copy(part, part, e_recv.at[(g + k) % NB, t]).wait()

            finish(recvx, fext, wfext, NX, 0, t)

    def take(slot, cb, chunk):
        @pl.loop(0, NT)
        def _(t):
            part = mrecv.at[slot, :, part_rows(t)]
            pltpu.make_async_copy(part, part, m_recv.at[slot, t]).wait()

        lanes = chunk_lanes(chunk)
        rg_ref[cb, :, lanes] = jnp.transpose(mrecv[slot, 0].astype(f32))
        se_ref[cb, :, lanes] = jnp.transpose(mrecv[slot, 1].astype(f32))

    @pl.when(jnp.logical_not(diag))
    def _():
        @pl.loop(0, NX)
        def _(k):
            take(k, 1 - own_cb, k)

    @pl.when(diag)
    def _():
        chunks = 4 + jnp.where(fifth, 1, 0)

        @pl.loop(0, 2 * NX)
        def _(d):
            taken = jnp.int32(0)
            for k in range(NX + 1):
                hit = ((code >> (4 * k)) & 7) == d
                taken = taken + jnp.where(jnp.logical_and(hit, k < chunks), 1, 0)

            @pl.when(taken == 0)
            def _():
                take(d, jnp.where(d >= NX, r, other), d % NX)

    @pl.loop(1, NQ)
    def _(k):
        y_copy(k).wait_send()

    core_copy(stage.at[y], stage.at[T_OTHER], 0).wait_send()
    core_copy(z_ref, cbuf, 1).wait_send()

    @pl.loop(0, NX)
    def _(c):
        for way in range(2):
            row_copy(way, c).wait_send()
            far_copy(way, c).wait_send()

    @pl.loop(1, NB)
    def _(k):
        g_copy(k).wait_send()
        p = (g + k) % NB

        @pl.loop(0, NT)
        def _(t):
            pair_copy(p // NX, p % NX, t).wait_send()

    @pl.loop(0, NT)
    def _(t):
        @pl.loop(0, 2)
        def _(e):
            @pl.when(y * NX + fifth_x(e) != g)
            def _():
                extra_copy(e, t).wait_send()

        @pl.loop(0, NX)
        def _(j):
            @pl.when(sends(j))
            def _():
                mirror_copy(j, t).wait_send()

        @pl.when(fifth)
        def _():
            mirror_copy(NX, t).wait_send()


def per_device(ldscore, zscores):
    dma = pltpu.SemaphoreType.DMA
    out = jax.ShapeDtypeStruct((2, ROWS, TB), f32)
    rg, se = pl.pallas_call(
        kernel,
        out_shape=(out, out),
        in_specs=[pl.BlockSpec(memory_space=pltpu.VMEM)] * 2,
        out_specs=[pl.BlockSpec(memory_space=pltpu.VMEM)] * 2,
        scratch_shapes=[
            pltpu.VMEM((T_LD + 1, 8, LANE), f32),
            pltpu.VMEM((NB, T_LD + 1, 8, LANE), f32),
            pltpu.VMEM((SNP, LANE), f32),
            pltpu.VMEM((SNP, LANE), f32),
            pltpu.VMEM((NQ * NT, 1, LANE), f32),
            pltpu.VMEM((NQ * NX, 1, LANE), f32),
            pltpu.VMEM((R_POS + 1, NX, 1, LANE), f32),
            pltpu.VMEM((LANE, LANE), f32),
            pltpu.VMEM((LANE, LANE), f32),
            pltpu.VMEM((2, TROWS, TB), f32),
            pltpu.VMEM((TROWS, TB + LANE), f32),
            pltpu.VMEM((NQ, NT, SNP, LANE), bf16),
            pltpu.VMEM((SNP, TB), bf16),
            pltpu.VMEM((2, SNP, TB), bf16),
            pltpu.VMEM((SNP, 2 * LANE), bf16),
            pltpu.VMEM((NB, 2, ROWS, TB), bf16),
            pltpu.VMEM((2, 2, ROWS, LANE), bf16),
            pltpu.VMEM((NB, 2, ROWS, TB), bf16),
            pltpu.VMEM((NB, 2, ROWS, LANE), bf16),
            pltpu.VMEM((3 * ROWS, SNP), bf16),
            pltpu.VMEM((SNP, TB), bf16),
            pltpu.VMEM((NB, 3 * ROWS, TB), f32),
            pltpu.VMEM((NB, 3 * ROWS, LANE), f32),
            pltpu.VMEM((NB, 2 * ROWS, TB), f32),
            pltpu.VMEM((NB, 2 * ROWS, LANE), f32),
            pltpu.VMEM((2, ROWS, TB), f32),
            pltpu.VMEM((2, ROWS, LANE), f32),
            pltpu.VMEM((NX + 1, 2, LANE, LANE), bf16),
            pltpu.VMEM((2 * NX, 2, LANE, LANE), bf16),
            dma((NQ,)),
            dma((NQ,)),
            dma((NB,)),
            dma((NB,)),
            dma((2,)),
            dma((2,)),
            dma((2, NT)),
            dma((2, NT)),
            dma((2, NT)),
            dma((2, NT)),
            dma((NB, NT)),
            dma((NB, NT)),
            dma((2, NT)),
            dma((NB, NT)),
            dma((NX + 1, NT)),
            dma((2 * NX, NT)),
        ],
        compiler_params=pltpu.CompilerParams(
            collective_id=0, has_side_effects=True, vmem_limit_bytes=56 * 1024 * 1024
        ),
    )(ldscore.reshape(8, LANE), zscores)
    return (rg.transpose(1, 0, 2)[None], se.transpose(1, 0, 2)[None])


def solution(mesh):
    return jax.shard_map(
        per_device,
        mesh=mesh,
        in_specs=(P("genome"), P("genome", ("trow", "tcol"))),
        out_specs=(P("trow", "genome", None, "tcol"), P("trow", "genome", None, "tcol")),
        check_vma=False,
    )
```

```python
import functools

import jax
import jax.numpy as jnp
from jax import lax
from jax.experimental import pallas as pl
from jax.experimental.pallas import tpu as pltpu
from jax.sharding import PartitionSpec as P

floor_value = 0.002
MESH = pl.DeviceIdType.MESH
f32 = jnp.float32
bf16 = jnp.bfloat16

SNP = 1024
TB = 512
LANE = 128
NCH = SNP // LANE
NB = 16
NQ = 4
NX = 4
ROWS = 128

R_FULL = NB
R_POS = NB + 1
TROWS = 24

T_OTHER = NQ
T_LD = NQ + 1

W_STEP = 4

NT = 4
PART = ROWS // NT
ORDER = (
    (2, 2), (1, 1), (3, 3), (1, 3), (3, 1), (1, 2), (3, 2), (2, 1), (2, 3),
    (0, 1), (1, 0), (0, 3), (3, 0), (0, 2), (2, 0),
)

DIAG = (
    ((3, 4, 5, 6), (1, 2, 5, 6, 7), (0, 1, 6, 7, 2), (0, 1, 7, 4)),
    ((0, 1, 4, 5, 6), (0, 5, 6, 7), (0, 3, 6, 7), (1, 2, 7, 4, 3)),
)


def digits(chunks):
    return sum(d << (4 * i) for i, d in enumerate(chunks))


def recip(value):
    return 1.0 / value


def column_tile(tile):
    return jnp.transpose(jnp.concatenate([tile] * (LANE // 8), axis=0))


def kernel(
    ld_ref,
    z_ref,
    rg_ref,
    se_ref,
    stage,
    allst,
    ldcol,
    lwcol,
    hrow,
    hpos,
    hdq,
    hdr,
    hdt,
    hcols,
    ctab,
    rbuf,
    cbuf,
    colw,
    lhsy,
    sendy,
    sendx,
    recvy,
    recvx,
    lhsw,
    ucol,
    wbuf,
    wext,
    fbuf,
    fext,
    wfull,
    wfext,
    msend,
    mrecv,
    y_send,
    y_recv,
    g_send,
    g_recv,
    c_send,
    c_recv,
    r_send,
    r_recv,
    f_send,
    f_recv,
    a_send,
    a_recv,
    e_send,
    e_recv,
    m_send,
    m_recv,
):
    g = lax.axis_index("genome")
    r = lax.axis_index("trow")
    y = lax.axis_index("tcol")
    zz = g // NX
    x = g % NX
    other = 1 - r
    diag = zz == y
    own_cb = jnp.where(zz > y, other, r)
    code = jnp.int32(0)
    for core in range(2):
        for at_x in range(NX):
            here = jnp.logical_and(r == core, x == at_x)
            code = jnp.where(here, digits(DIAG[core][at_x]), code)
    fifth = jnp.logical_and(diag, ((x + 1) // 2 + r) % 2 == 1)

    barrier = pltpu.get_barrier_semaphore()

    def greet(dev):
        pl.semaphore_signal(barrier, inc=1, device_id=dev, device_id_type=MESH)

    @pl.loop(1, NB)
    def _(k):
        greet(((g + k) % NB, r, y))

    @pl.loop(1, NQ)
    def _(k):
        greet((g, r, (y + k) % NQ))

    greet((g, other, y))

    @pl.when(diag)
    def _():
        @pl.loop(0, NX)
        def _(k):
            greet((zz * NX + k, other, y))

    @pl.when(jnp.logical_not(diag))
    def _():
        @pl.loop(0, NX)
        def _(k):
            greet((y * NX + k, r, zz))
            greet((y * NX + k, other, zz))

    ld_tile = ld_ref[...]
    ld_t = column_tile(ld_tile)
    for c in range(NCH):
        col = jnp.broadcast_to(ld_t[:, c : c + 1], (LANE, LANE))
        ldcol[c * LANE : (c + 1) * LANE, :] = col
        lwcol[c * LANE : (c + 1) * LANE, :] = recip(col)
    for c in range(TB // LANE):
        lanes = slice(c * LANE, (c + 1) * LANE)
        acc_y = jnp.zeros((8, LANE), f32)
        acc_l = jnp.zeros((8, LANE), f32)
        for s in range(NCH):
            rows = slice(s * LANE, (s + 1) * LANE)
            zc = z_ref[rows, lanes].astype(f32)
            sq = zc * zc
            acc_l = acc_l + jnp.sum(sq.reshape(LANE // 8, 8, LANE), axis=0)
            acc_y = acc_y + jnp.sum((sq * lwcol[rows, :]).reshape(LANE // 8, 8, LANE), axis=0)
        stage[y, c : c + 1, :] = jnp.sum(acc_y, axis=0, keepdims=True)
        stage[y, 4 + c : 5 + c, :] = jnp.sum(acc_l, axis=0, keepdims=True)
    stage[T_LD] = ld_tile

    def gather_parts(value, t):
        return jnp.concatenate(
            [value[:, c * LANE + t * PART : c * LANE + (t + 1) * PART] for c in range(NX)], axis=1
        )

    def make_chunk(t):
        for s in range(NCH):
            rows = slice(s * LANE, (s + 1) * LANE)
            rbuf[y, t, rows, :] = gather_parts(z_ref[rows, :], t)

    make_chunk(0)

    @pl.when(diag)
    def _():
        pl.semaphore_wait(barrier, NB - 1 + NQ - 1 + 1 + NX)

    @pl.when(jnp.logical_not(diag))
    def _():
        pl.semaphore_wait(barrier, NB - 1 + NQ - 1 + 1 + 2 * NX)

    def y_copy(k):
        return pltpu.make_async_remote_copy(
            src_ref=stage.at[y],
            dst_ref=stage.at[y],
            send_sem=y_send.at[k],
            recv_sem=y_recv.at[y],
            device_id=(g, r, (y + k) % NQ),
            device_id_type=MESH,
        )

    def core_copy(src, dst, i):
        return pltpu.make_async_remote_copy(
            src_ref=src,
            dst_ref=dst,
            send_sem=c_send.at[i],
            recv_sem=c_recv.at[i],
            device_id=(g, other, y),
            device_id_type=MESH,
        )

    @pl.loop(1, NQ)
    def _(k):
        y_copy(k).start()

    core_copy(stage.at[y], stage.at[T_OTHER], 0).start()
    core_copy(z_ref, cbuf, 1).start()

    def row_copy(way, c):
        return pltpu.make_async_remote_copy(
            src_ref=rbuf.at[y, c],
            dst_ref=rbuf.at[y, c],
            send_sem=r_send.at[way, c],
            recv_sem=r_recv.at[way, c],
            device_id=(g, r, (y + 1 + 2 * way) % NQ),
            device_id_type=MESH,
        )

    def far_copy(way, c):
        q = (y + 3 + 2 * way) % NQ
        part = rbuf.at[q, c, pl.ds(pl.multiple_of(way * (SNP // 2), SNP // 2), SNP // 2)]
        return pltpu.make_async_remote_copy(
            src_ref=part,
            dst_ref=part,
            send_sem=f_send.at[way, c],
            recv_sem=f_recv.at[way, c],
            device_id=(g, r, (y + 1 + 2 * way) % NQ),
            device_id_type=MESH,
        )

    def send_chunk(step):
        row_copy(0, step).start()
        row_copy(1, step).start()

    def pass_on(step):
        for way in range(2):
            q = (y + 3 + 2 * way) % NQ
            pltpu.make_async_copy(
                rbuf.at[q, step], rbuf.at[q, step], r_recv.at[way, step]
            ).wait()
            far_copy(way, step).start()

    send_chunk(0)
    make_chunk(1)

    @pl.loop(1, NQ)
    def _(k):
        q = (y + k) % NQ
        pltpu.make_async_copy(stage.at[q], stage.at[q], y_recv.at[q]).wait()

    pltpu.make_async_copy(stage.at[T_OTHER], stage.at[T_OTHER], c_recv.at[0]).wait()

    def g_copy(k):
        return pltpu.make_async_remote_copy(
            src_ref=stage,
            dst_ref=allst.at[g],
            send_sem=g_send.at[k],
            recv_sem=g_recv.at[g],
            device_id=((g + k) % NB, r, y),
            device_id_type=MESH,
        )

    @pl.loop(1, NB)
    def _(k):
        g_copy(k).start()

    allst[g] = stage[...]
    make_chunk(2)
    make_chunk(3)
    pass_on(0)

    @pl.loop(1, NB)
    def _(k):
        b = (g + k) % NB
        pltpu.make_async_copy(allst.at[b], allst.at[b], g_recv.at[b]).wait()

    inv_b = []
    lds_b = []
    for b in range(NB):
        tile = allst[b, T_LD]
        inv_b.append(jnp.sum(jnp.sum(recip(tile), axis=0, keepdims=True), axis=1, keepdims=True))
        lds_b.append(jnp.sum(jnp.sum(tile, axis=0, keepdims=True), axis=1, keepdims=True))
    inv_t = functools.reduce(jnp.add, inv_b)
    lds_t = functools.reduce(jnp.add, lds_b)

    def slope(inv, ld, sums, count):
        return (inv * sums[4:8] - count * sums[0:4]) / (inv * ld - count * count)

    n_full = float(SNP * NB)
    n_del = float(SNP * (NB - 1))

    def total_of(q):
        total = allst[0, q]
        for b in range(1, NB):
            total = total + allst[b, q]
        return total

    def scaled(h):
        return lax.rsqrt(jnp.maximum(h, floor_value))

    for q in range(NQ):
        h = jnp.maximum(slope(inv_t, lds_t, total_of(q), n_full), 0.0)
        for c in range(NX):
            hpos[q * NX + c] = h[c : c + 1, :]
        for t in range(NT):
            hrow[q * NT + t] = jnp.concatenate(
                [h[c : c + 1, t * PART : (t + 1) * PART] for c in range(NX)], axis=1
            )

    for cb, q in ((r, y), (other, T_OTHER)):
        h_full = slope(inv_t, lds_t, total_of(q), n_full)
        hcols[cb, TROWS - 8 : TROWS, :] = jnp.zeros((8, TB), f32)
        for c in range(NX):
            lanes = slice(c * LANE, (c + 1) * LANE)
            hcols[cb, R_FULL : R_FULL + 1, lanes] = scaled(h_full[c : c + 1, :])
            hcols[cb, R_POS : R_POS + 1, lanes] = jnp.maximum(h_full[c : c + 1, :], 0.0)

    def weigh_columns(src, cb):
        @pl.loop(0, NCH)
        def _(s):
            rows = pl.ds(pl.multiple_of(s * LANE, LANE), LANE)
            for c in range(TB // LANE):
                lanes = slice(c * LANE, (c + 1) * LANE)
                h = hcols[cb, R_POS : R_POS + 1, lanes]
                u = recip(1.0 + h * ldcol[rows, :]).astype(bf16).astype(f32)
                colw[cb, rows, lanes] = (src[rows, lanes].astype(f32) * u).astype(bf16)

    weigh_columns(z_ref, r)
    pltpu.make_async_copy(cbuf, cbuf, c_recv.at[1]).wait()
    weigh_columns(cbuf, other)

    send_chunk(1)

    def part_rows(t):
        return pl.ds(pl.multiple_of(t * PART, PART), PART)

    def pair_copy(q, c, t):
        return pltpu.make_async_remote_copy(
            src_ref=sendy.at[q * NX + c, :, part_rows(t)],
            dst_ref=recvy.at[g, :, part_rows(t)],
            send_sem=a_send.at[q * NX + c, t],
            recv_sem=a_recv.at[g, t],
            device_id=(q * NX + c, r, y),
            device_id_type=MESH,
        )

    def fifth_x(e):
        return jnp.where(r == 0, 1 + e, 3 * e)

    def extra_copy(e, t):
        return pltpu.make_async_remote_copy(
            src_ref=sendx.at[e, :, part_rows(t)],
            dst_ref=recvx.at[g, :, part_rows(t)],
            send_sem=e_send.at[e, t],
            recv_sem=e_recv.at[g, t],
            device_id=(y * NX + fifth_x(e), r, y),
            device_id_type=MESH,
        )

    def contract(left, right):
        return lax.dot_general(left, right, (((0,), (0,)), ((), ())), preferred_element_type=f32)

    def chunk_lanes(c):
        return pl.ds(pl.multiple_of((c % NX) * LANE, LANE), LANE)

    def weigh_rows(q, t):
        h = hrow[q * NT + t]
        for s in range(NCH):
            rows = slice(s * LANE, (s + 1) * LANE)
            u = recip(1.0 + h * ldcol[rows, :]).astype(bf16).astype(f32)
            value = rbuf[q, t, rows, :].astype(f32) * u
            lhsy[rows, 0:LANE] = (value * lwcol[rows, :]).astype(bf16)
            lhsy[rows, LANE : 2 * LANE] = value.astype(bf16)

    def pair_sums(q, t):
        weigh_rows(q, t)
        cb = jnp.where(q > y, other, r)
        sums = contract(lhsy[...], colw[cb]).astype(bf16)
        for c in range(NX):
            for i in range(2):
                first = i * LANE + c * PART
                sendy[q * NX + c, i, part_rows(t), :] = sums[first : first + PART]

    def own_sums(t):
        weigh_rows(y, t)
        sums = (
            contract(lhsy[...], colw[other]).astype(bf16),
            contract(lhsy[...], colw[r]).astype(bf16),
        )

        def piece(core, c, k, i):
            d = DIAG[core][c][k]
            rows = slice(i * LANE + c * PART, i * LANE + (c + 1) * PART)
            return sums[d // NX][rows, d % NX * LANE : (d % NX + 1) * LANE]

        def pick(zero, one):
            return jnp.where(r == 0, zero.astype(f32), one.astype(f32)).astype(bf16)

        for i in range(2):
            for c in range(NX):
                for k in range(4):
                    sendy[y * NX + c, i, part_rows(t), k * LANE : (k + 1) * LANE] = pick(
                        piece(0, c, k, i), piece(1, c, k, i)
                    )
            for e in range(2):
                sendx[e, i, part_rows(t), :] = pick(piece(0, 1 + e, 4, i), piece(1, 3 * e, 4, i))

    def deliver(t):
        for dz, dx in ORDER:
            pair_copy((zz + dz) % NQ, (x + dx) % NX, t).start()

        recvy[g, :, part_rows(t), :] = sendy[g, :, part_rows(t), :]

        @pl.loop(0, 2)
        def _(e):
            @pl.when(y * NX + fifth_x(e) == g)
            def _():
                recvx[g, :, part_rows(t), :] = sendx[e, :, part_rows(t), :]

            @pl.when(y * NX + fifth_x(e) != g)
            def _():
                extra_copy(e, t).start()

    def place(j):
        d = (code >> (4 * j)) & 7
        cb = jnp.where(diag, jnp.where(d >= NX, r, other), own_cb)
        return cb, jnp.where(diag, d % NX, j % NX)

    def make_table(rows):
        for k in range(NX + 1):
            cb, chunk = place(k)
            ctab[rows, k * LANE : (k + 1) * LANE] = hcols[cb, rows, chunk_lanes(chunk)]

    make_table(slice(TROWS - 8, TROWS))
    hdr[...] = jnp.zeros((LANE, LANE), f32)
    hdr[R_POS : R_POS + 1, :] = hpos[zz * NX + x]
    hdt[...] = jnp.transpose(hdr[...])

    def weight_sums(b):
        tile = allst[b, T_LD]
        inv = recip(tile)
        h = hdt[:, R_POS : R_POS + 1]
        for c in range(NCH):
            lanes = slice(c * LANE, (c + 1) * LANE)
            row = tile[c : c + 1, :]
            u16 = recip(1.0 + h * row).astype(bf16)
            u = u16.astype(f32)
            lhsw[0:ROWS, lanes] = (u * inv[c : c + 1, :]).astype(bf16)
            lhsw[ROWS : 2 * ROWS, lanes] = u16
            lhsw[2 * ROWS : 3 * ROWS, lanes] = (u * row).astype(bf16)
        ldc = column_tile(tile)
        h = ctab[R_POS : R_POS + 1, 0:TB]
        for c in range(NCH):
            ucol[c * LANE : (c + 1) * LANE, :] = recip(1.0 + ldc[:, c : c + 1] * h).astype(bf16)
        wbuf[b] = jnp.dot(lhsw[...], ucol[...], preferred_element_type=f32)

        @pl.when(fifth)
        def _():
            h = ctab[R_POS : R_POS + 1, TB : TB + LANE]
            for c in range(NCH):
                ucol[c * LANE : (c + 1) * LANE, 0:LANE] = recip(1.0 + ldc[:, c : c + 1] * h).astype(
                    bf16
                )
            wext[b] = jnp.dot(lhsw[...], ucol[:, 0:LANE], preferred_element_type=f32)

    @pl.loop(0, NX)
    def _(step):
        far = (y + 2) % NQ
        for way in range(2):
            part = rbuf.at[far, step, pl.ds(way * (SNP // 2), SNP // 2)]
            pltpu.make_async_copy(part, part, f_recv.at[way, step]).wait()

        @pl.loop(0, NQ)
        def _(k):
            @pl.when(k == y)
            def _():
                own_sums(step)

            @pl.when(k != y)
            def _():
                pair_sums(k, step)

        deliver(step)

        @pl.when(step < NT - 1)
        def _():
            pass_on(step + 1)

        @pl.when(step < NT - 2)
        def _():
            send_chunk(step + 2)

        @pl.loop(0, W_STEP)
        def _(k):
            weight_sums(step * W_STEP + k)


    @pl.loop(NT * W_STEP, NB)
    def _(b):
        weight_sums(b)

    for cb, q in ((r, y), (other, T_OTHER)):
        total = total_of(q)
        for b in range(NB):
            h = scaled(slope(inv_t - inv_b[b], lds_t - lds_b[b], total - allst[b, q], n_del))
            for c in range(NX):
                hcols[cb, b : b + 1, c * LANE : (c + 1) * LANE] = h[c : c + 1, :]
    make_table(slice(0, NB))
    total = total_of(zz)
    h_full = scaled(slope(inv_t, lds_t, total, n_full))
    for c in range(NX):
        hdq[R_FULL, c] = h_full[c : c + 1, :]
    for b in range(NB):
        h = scaled(slope(inv_t - inv_b[b], lds_t - lds_b[b], total - allst[b, zz], n_del))
        for c in range(NX):
            hdq[b, c] = h[c : c + 1, :]
    for b in range(NB + 1):
        hdr[b : b + 1, :] = hdq[b, x]
    hdt[...] = jnp.transpose(hdr[...])

    def factors(weights, parts, full, first, width):
        @pl.loop(0, ROWS // 8)
        def _(t):
            base = pl.multiple_of(t * 8, 8)

            def at(i):
                return pl.ds(i * ROWS + base, 8)

            for c in range(width // LANE):
                lanes = slice(c * LANE, (c + 1) * LANE)
                tlanes = slice(first + c * LANE, first + (c + 1) * LANE)
                tot = [weights[0, at(i), lanes] for i in range(3)]
                for b in range(1, NB):
                    tot = [tot[i] + weights[b, at(i), lanes] for i in range(3)]

                def pair(w, b):
                    scale = hdt[pl.ds(base, 8), b : b + 1] * ctab[b : b + 1, tlanes]
                    k = scale / (w[0] * w[2] - w[1] * w[1])
                    return w[0] * k, w[1] * k

                full[0, pl.ds(base, 8), lanes], full[1, pl.ds(base, 8), lanes] = pair(tot, R_FULL)
                for b in range(NB):
                    w = [tot[i] - weights[b, at(i), lanes] for i in range(3)]
                    parts[b, at(0), lanes], parts[b, at(1), lanes] = pair(w, b)

    factors(wbuf, fbuf, wfull, 0, TB)

    @pl.when(fifth)
    def _():
        factors(wext, fext, wfext, TB, LANE)

    def mirror_copy(j, t):
        cb, chunk = place(j)
        slot = jnp.where(jnp.logical_and(diag, cb == r), NX + x, x)
        return pltpu.make_async_remote_copy(
            src_ref=msend.at[j, :, part_rows(t)],
            dst_ref=mrecv.at[slot, :, part_rows(t)],
            send_sem=m_send.at[j, t],
            recv_sem=m_recv.at[slot, t],
            device_id=(y * NX + chunk, cb, zz),
            device_id_type=MESH,
        )

    def sends(j):
        cb, chunk = place(j)
        return jnp.logical_not(diag & (cb == r) & (chunk == x))

    def finish(pairs, weights, full, j, first, t):
        cb, chunk = place(j)
        out = chunk_lanes(chunk)
        lanes = pl.ds(pl.multiple_of(first, LANE), LANE)

        @pl.loop(0, PART // 16)
        def _(i):
            base = pl.multiple_of(t * PART + i * 16, 16)
            rows = pl.ds(base, 16)
            tot0 = pairs[0, 0, rows, lanes].astype(f32)
            tot1 = pairs[0, 1, rows, lanes].astype(f32)
            for b in range(1, NB):
                tot0 = tot0 + pairs[b, 0, rows, lanes].astype(f32)
                tot1 = tot1 + pairs[b, 1, rows, lanes].astype(f32)
            rg = full[0, rows, lanes] * tot1 - full[1, rows, lanes] * tot0
            rg_ref[cb, rows, out] = rg
            msend[j, 0, rows, :] = rg.astype(bf16)
            values = []
            for b in range(NB):
                del0 = tot0 - pairs[b, 0, rows, lanes].astype(f32)
                del1 = tot1 - pairs[b, 1, rows, lanes].astype(f32)
                values.append(
                    weights[b, pl.ds(base, 16), lanes] * del1
                    - weights[b, pl.ds(ROWS + base, 16), lanes] * del0
                )
            mean = functools.reduce(jnp.add, values) * (1.0 / NB)
            spread = functools.reduce(jnp.add, [(v - mean) * (v - mean) for v in values])
            se = jnp.sqrt((NB - 1) / NB * spread)
            se_ref[cb, rows, out] = se
            msend[j, 1, rows, :] = se.astype(bf16)

        @pl.when(sends(j))
        def _():
            mirror_copy(j, t).start()

    @pl.loop(0, NT)
    def _(t):
        @pl.loop(1, NB)
        def _(k):
            part = recvy.at[(g + k) % NB, :, part_rows(t)]
            pltpu.make_async_copy(part, part, a_recv.at[(g + k) % NB, t]).wait()

        @pl.loop(0, NX)
        def _(j):
            finish(recvy, fbuf, wfull, j, j * LANE, t)

        @pl.when(fifth)
        def _():
            @pl.loop(1, NB)
            def _(k):
                part = recvx.at[(g + k) % NB, :, part_rows(t)]
                pltpu.make_async_copy(part, part, e_recv.at[(g + k) % NB, t]).wait()

            finish(recvx, fext, wfext, NX, 0, t)

    def take(slot, cb, chunk):
        @pl.loop(0, NT)
        def _(t):
            part = mrecv.at[slot, :, part_rows(t)]
            pltpu.make_async_copy(part, part, m_recv.at[slot, t]).wait()

        lanes = chunk_lanes(chunk)
        rg_ref[cb, :, lanes] = jnp.transpose(mrecv[slot, 0].astype(f32))
        se_ref[cb, :, lanes] = jnp.transpose(mrecv[slot, 1].astype(f32))

    @pl.when(jnp.logical_not(diag))
    def _():
        @pl.loop(0, NX)
        def _(k):
            take(k, 1 - own_cb, k)

    @pl.when(diag)
    def _():
        chunks = 4 + jnp.where(fifth, 1, 0)

        @pl.loop(0, 2 * NX)
        def _(d):
            taken = jnp.int32(0)
            for k in range(NX + 1):
                hit = ((code >> (4 * k)) & 7) == d
                taken = taken + jnp.where(jnp.logical_and(hit, k < chunks), 1, 0)

            @pl.when(taken == 0)
            def _():
                take(d, jnp.where(d >= NX, r, other), d % NX)

    @pl.loop(1, NQ)
    def _(k):
        y_copy(k).wait_send()

    core_copy(stage.at[y], stage.at[T_OTHER], 0).wait_send()
    core_copy(z_ref, cbuf, 1).wait_send()

    @pl.loop(0, NX)
    def _(c):
        for way in range(2):
            row_copy(way, c).wait_send()
            far_copy(way, c).wait_send()

    @pl.loop(1, NB)
    def _(k):
        g_copy(k).wait_send()
        p = (g + k) % NB

        @pl.loop(0, NT)
        def _(t):
            pair_copy(p // NX, p % NX, t).wait_send()

    @pl.loop(0, NT)
    def _(t):
        @pl.loop(0, 2)
        def _(e):
            @pl.when(y * NX + fifth_x(e) != g)
            def _():
                extra_copy(e, t).wait_send()

        @pl.loop(0, NX)
        def _(j):
            @pl.when(sends(j))
            def _():
                mirror_copy(j, t).wait_send()

        @pl.when(fifth)
        def _():
            mirror_copy(NX, t).wait_send()


def per_device(ldscore, zscores):
    dma = pltpu.SemaphoreType.DMA
    out = jax.ShapeDtypeStruct((2, ROWS, TB), f32)
    rg, se = pl.pallas_call(
        kernel,
        out_shape=(out, out),
        in_specs=[pl.BlockSpec(memory_space=pltpu.VMEM)] * 2,
        out_specs=[pl.BlockSpec(memory_space=pltpu.VMEM)] * 2,
        scratch_shapes=[
            pltpu.VMEM((T_LD + 1, 8, LANE), f32),
            pltpu.VMEM((NB, T_LD + 1, 8, LANE), f32),
            pltpu.VMEM((SNP, LANE), f32),
            pltpu.VMEM((SNP, LANE), f32),
            pltpu.VMEM((NQ * NT, 1, LANE), f32),
            pltpu.VMEM((NQ * NX, 1, LANE), f32),
            pltpu.VMEM((R_POS + 1, NX, 1, LANE), f32),
            pltpu.VMEM((LANE, LANE), f32),
            pltpu.VMEM((LANE, LANE), f32),
            pltpu.VMEM((2, TROWS, TB), f32),
            pltpu.VMEM((TROWS, TB + LANE), f32),
            pltpu.VMEM((NQ, NT, SNP, LANE), bf16),
            pltpu.VMEM((SNP, TB), bf16),
            pltpu.VMEM((2, SNP, TB), bf16),
            pltpu.VMEM((SNP, 2 * LANE), bf16),
            pltpu.VMEM((NB, 2, ROWS, TB), bf16),
            pltpu.VMEM((2, 2, ROWS, LANE), bf16),
            pltpu.VMEM((NB, 2, ROWS, TB), bf16),
            pltpu.VMEM((NB, 2, ROWS, LANE), bf16),
            pltpu.VMEM((3 * ROWS, SNP), bf16),
            pltpu.VMEM((SNP, TB), bf16),
            pltpu.VMEM((NB, 3 * ROWS, TB), f32),
            pltpu.VMEM((NB, 3 * ROWS, LANE), f32),
            pltpu.VMEM((NB, 2 * ROWS, TB), f32),
            pltpu.VMEM((NB, 2 * ROWS, LANE), f32),
            pltpu.VMEM((2, ROWS, TB), f32),
            pltpu.VMEM((2, ROWS, LANE), f32),
            pltpu.VMEM((NX + 1, 2, LANE, LANE), bf16),
            pltpu.VMEM((2 * NX, 2, LANE, LANE), bf16),
            dma((NQ,)),
            dma((NQ,)),
            dma((NB,)),
            dma((NB,)),
            dma((2,)),
            dma((2,)),
            dma((2, NT)),
            dma((2, NT)),
            dma((2, NT)),
            dma((2, NT)),
            dma((NB, NT)),
            dma((NB, NT)),
            dma((2, NT)),
            dma((NB, NT)),
            dma((NX + 1, NT)),
            dma((2 * NX, NT)),
        ],
        compiler_params=pltpu.CompilerParams(
            collective_id=0, has_side_effects=True, vmem_limit_bytes=56 * 1024 * 1024
        ),
    )(ldscore.reshape(8, LANE), zscores)
    return (rg.transpose(1, 0, 2)[None], se.transpose(1, 0, 2)[None])


def solution(mesh):
    return jax.shard_map(
        per_device,
        mesh=mesh,
        in_specs=(P("genome"), P("genome", ("trow", "tcol"))),
        out_specs=(P("trow", "genome", None, "tcol"), P("trow", "genome", None, "tcol")),
        check_vma=False,
    )
```

```python
import functools

import jax
import jax.numpy as jnp
from jax import lax
from jax.experimental import pallas as pl
from jax.experimental.pallas import tpu as pltpu
from jax.sharding import PartitionSpec as P

floor_value = 0.002
MESH = pl.DeviceIdType.MESH
f32 = jnp.float32
bf16 = jnp.bfloat16

SNP = 1024
TB = 512
LANE = 128
NCH = SNP // LANE
NB = 16
NQ = 4
NX = 4
ROWS = 128

R_FULL = NB
R_POS = NB + 1
TROWS = 24

T_OTHER = NQ
T_LD = NQ + 1

W_STEP = 4

NT = 4
PART = ROWS // NT
ORDER = (
    (2, 2), (1, 1), (3, 3), (1, 3), (3, 1), (1, 2), (3, 2), (2, 1), (2, 3),
    (0, 1), (1, 0), (0, 3), (3, 0), (0, 2), (2, 0),
)

DIAG = (
    ((3, 4, 5, 6), (1, 2, 5, 6, 7), (0, 1, 6, 7, 2), (0, 1, 7, 4)),
    ((0, 1, 4, 5, 6), (0, 5, 6, 7), (0, 3, 6, 7), (1, 2, 7, 4, 3)),
)


def digits(chunks):
    return sum(d << (4 * i) for i, d in enumerate(chunks))


def recip(value):
    return 1.0 / value


def column_tile(tile):
    return jnp.transpose(jnp.concatenate([tile] * (LANE // 8), axis=0))


def kernel(
    ld_ref,
    z_ref,
    rg_ref,
    se_ref,
    stage,
    allst,
    ldcol,
    lwcol,
    hrow,
    hpos,
    hdq,
    hdr,
    hdt,
    hcols,
    ctab,
    rbuf,
    cbuf,
    colw,
    lhsy,
    sendy,
    sendx,
    recvy,
    recvx,
    lhsw,
    ucol,
    wbuf,
    wext,
    fbuf,
    fext,
    wfull,
    wfext,
    msend,
    mrecv,
    y_send,
    y_recv,
    g_send,
    g_recv,
    c_send,
    c_recv,
    r_send,
    r_recv,
    f_send,
    f_recv,
    a_send,
    a_recv,
    e_send,
    e_recv,
    m_send,
    m_recv,
):
    g = lax.axis_index("genome")
    r = lax.axis_index("trow")
    y = lax.axis_index("tcol")
    zz = g // NX
    x = g % NX
    other = 1 - r
    diag = zz == y
    own_cb = jnp.where(zz > y, other, r)
    code = jnp.int32(0)
    for core in range(2):
        for at_x in range(NX):
            here = jnp.logical_and(r == core, x == at_x)
            code = jnp.where(here, digits(DIAG[core][at_x]), code)
    fifth = jnp.logical_and(diag, ((x + 1) // 2 + r) % 2 == 1)

    barrier = pltpu.get_barrier_semaphore()

    def greet(dev):
        pl.semaphore_signal(barrier, inc=1, device_id=dev, device_id_type=MESH)

    @pl.loop(1, NB)
    def _(k):
        greet(((g + k) % NB, r, y))

    @pl.loop(1, NQ)
    def _(k):
        greet((g, r, (y + k) % NQ))

    greet((g, other, y))

    @pl.when(diag)
    def _():
        @pl.loop(0, NX)
        def _(k):
            greet((zz * NX + k, other, y))

    @pl.when(jnp.logical_not(diag))
    def _():
        @pl.loop(0, NX)
        def _(k):
            greet((y * NX + k, r, zz))
            greet((y * NX + k, other, zz))

    ld_tile = ld_ref[...]
    ld_t = column_tile(ld_tile)
    for c in range(NCH):
        col = jnp.broadcast_to(ld_t[:, c : c + 1], (LANE, LANE))
        ldcol[c * LANE : (c + 1) * LANE, :] = col
        lwcol[c * LANE : (c + 1) * LANE, :] = recip(col)
    for c in range(TB // LANE):
        lanes = slice(c * LANE, (c + 1) * LANE)
        acc_y = jnp.zeros((8, LANE), f32)
        acc_l = jnp.zeros((8, LANE), f32)
        for s in range(NCH):
            rows = slice(s * LANE, (s + 1) * LANE)
            zc = z_ref[rows, lanes].astype(f32)
            sq = zc * zc
            acc_l = acc_l + jnp.sum(sq.reshape(LANE // 8, 8, LANE), axis=0)
            acc_y = acc_y + jnp.sum((sq * lwcol[rows, :]).reshape(LANE // 8, 8, LANE), axis=0)
        stage[y, c : c + 1, :] = jnp.sum(acc_y, axis=0, keepdims=True)
        stage[y, 4 + c : 5 + c, :] = jnp.sum(acc_l, axis=0, keepdims=True)
    stage[T_LD] = ld_tile

    def gather_parts(value, t):
        return jnp.concatenate(
            [value[:, c * LANE + t * PART : c * LANE + (t + 1) * PART] for c in range(NX)], axis=1
        )

    def make_chunk(t):
        for s in range(NCH):
            rows = slice(s * LANE, (s + 1) * LANE)
            rbuf[y, t, rows, :] = gather_parts(z_ref[rows, :], t)

    make_chunk(0)

    @pl.when(diag)
    def _():
        pl.semaphore_wait(barrier, NB - 1 + NQ - 1 + 1 + NX)

    @pl.when(jnp.logical_not(diag))
    def _():
        pl.semaphore_wait(barrier, NB - 1 + NQ - 1 + 1 + 2 * NX)

    def y_copy(k):
        return pltpu.make_async_remote_copy(
            src_ref=stage.at[y],
            dst_ref=stage.at[y],
            send_sem=y_send.at[k],
            recv_sem=y_recv.at[y],
            device_id=(g, r, (y + k) % NQ),
            device_id_type=MESH,
        )

    def core_copy(src, dst, i):
        return pltpu.make_async_remote_copy(
            src_ref=src,
            dst_ref=dst,
            send_sem=c_send.at[i],
            recv_sem=c_recv.at[i],
            device_id=(g, other, y),
            device_id_type=MESH,
        )

    @pl.loop(1, NQ)
    def _(k):
        y_copy(k).start()

    core_copy(stage.at[y], stage.at[T_OTHER], 0).start()
    core_copy(z_ref, cbuf, 1).start()

    def half_of(q, c, h):
        return rbuf.at[q, c, pl.ds(h * (SNP // 2), SNP // 2)]

    def row_copy(way, c, p):
        part = half_of(y, c, (way + p) % 2)
        return pltpu.make_async_remote_copy(
            src_ref=part,
            dst_ref=part,
            send_sem=r_send.at[way, p, c],
            recv_sem=r_recv.at[way, p, c],
            device_id=(g, r, (y + 1 + 2 * way) % NQ),
            device_id_type=MESH,
        )

    def far_copy(way, c):
        q = (y + 3 + 2 * way) % NQ
        part = rbuf.at[q, c, pl.ds(pl.multiple_of(way * (SNP // 2), SNP // 2), SNP // 2)]
        return pltpu.make_async_remote_copy(
            src_ref=part,
            dst_ref=part,
            send_sem=f_send.at[way, c],
            recv_sem=f_recv.at[way, c],
            device_id=(g, r, (y + 1 + 2 * way) % NQ),
            device_id_type=MESH,
        )

    def send_chunk(step, parts=(0, 1)):
        for p in parts:
            row_copy(0, step, p).start()
            row_copy(1, step, p).start()

    def pass_on(step):
        for way in range(2):
            q = (y + 3 + 2 * way) % NQ
            part = half_of(q, step, way)
            pltpu.make_async_copy(part, part, r_recv.at[way, 0, step]).wait()
            far_copy(way, step).start()

    send_chunk(0)
    make_chunk(1)

    @pl.loop(1, NQ)
    def _(k):
        q = (y + k) % NQ
        pltpu.make_async_copy(stage.at[q], stage.at[q], y_recv.at[q]).wait()

    pltpu.make_async_copy(stage.at[T_OTHER], stage.at[T_OTHER], c_recv.at[0]).wait()

    def g_copy(k):
        return pltpu.make_async_remote_copy(
            src_ref=stage,
            dst_ref=allst.at[g],
            send_sem=g_send.at[k],
            recv_sem=g_recv.at[g],
            device_id=((g + k) % NB, r, y),
            device_id_type=MESH,
        )

    @pl.loop(1, NB)
    def _(k):
        g_copy(k).start()

    allst[g] = stage[...]
    make_chunk(2)
    make_chunk(3)
    pass_on(0)

    @pl.loop(1, NB)
    def _(k):
        b = (g + k) % NB
        pltpu.make_async_copy(allst.at[b], allst.at[b], g_recv.at[b]).wait()

    inv_b = []
    lds_b = []
    for b in range(NB):
        tile = allst[b, T_LD]
        inv_b.append(jnp.sum(jnp.sum(recip(tile), axis=0, keepdims=True), axis=1, keepdims=True))
        lds_b.append(jnp.sum(jnp.sum(tile, axis=0, keepdims=True), axis=1, keepdims=True))
    inv_t = functools.reduce(jnp.add, inv_b)
    lds_t = functools.reduce(jnp.add, lds_b)

    def slope(inv, ld, sums, count):
        return (inv * sums[4:8] - count * sums[0:4]) / (inv * ld - count * count)

    n_full = float(SNP * NB)
    n_del = float(SNP * (NB - 1))

    def total_of(q):
        total = allst[0, q]
        for b in range(1, NB):
            total = total + allst[b, q]
        return total

    def scaled(h):
        return lax.rsqrt(jnp.maximum(h, floor_value))

    for q in range(NQ):
        h = jnp.maximum(slope(inv_t, lds_t, total_of(q), n_full), 0.0)
        for c in range(NX):
            hpos[q * NX + c] = h[c : c + 1, :]
        for t in range(NT):
            hrow[q * NT + t] = jnp.concatenate(
                [h[c : c + 1, t * PART : (t + 1) * PART] for c in range(NX)], axis=1
            )

    for cb, q in ((r, y), (other, T_OTHER)):
        h_full = slope(inv_t, lds_t, total_of(q), n_full)
        hcols[cb, TROWS - 8 : TROWS, :] = jnp.zeros((8, TB), f32)
        for c in range(NX):
            lanes = slice(c * LANE, (c + 1) * LANE)
            hcols[cb, R_FULL : R_FULL + 1, lanes] = scaled(h_full[c : c + 1, :])
            hcols[cb, R_POS : R_POS + 1, lanes] = jnp.maximum(h_full[c : c + 1, :], 0.0)

    def weigh_columns(src, cb):
        @pl.loop(0, NCH)
        def _(s):
            rows = pl.ds(pl.multiple_of(s * LANE, LANE), LANE)
            for c in range(TB // LANE):
                lanes = slice(c * LANE, (c + 1) * LANE)
                h = hcols[cb, R_POS : R_POS + 1, lanes]
                u = recip(1.0 + h * ldcol[rows, :]).astype(bf16).astype(f32)
                colw[cb, rows, lanes] = (src[rows, lanes].astype(f32) * u).astype(bf16)

    weigh_columns(z_ref, r)
    pltpu.make_async_copy(cbuf, cbuf, c_recv.at[1]).wait()
    weigh_columns(cbuf, other)

    send_chunk(1)

    def part_rows(t):
        return pl.ds(pl.multiple_of(t * PART, PART), PART)

    def pair_copy(q, c, t):
        return pltpu.make_async_remote_copy(
            src_ref=sendy.at[q * NX + c, :, part_rows(t)],
            dst_ref=recvy.at[g, :, part_rows(t)],
            send_sem=a_send.at[q * NX + c, t],
            recv_sem=a_recv.at[g, t],
            device_id=(q * NX + c, r, y),
            device_id_type=MESH,
        )

    def fifth_x(e):
        return jnp.where(r == 0, 1 + e, 3 * e)

    def extra_copy(e, t):
        return pltpu.make_async_remote_copy(
            src_ref=sendx.at[e, :, part_rows(t)],
            dst_ref=recvx.at[g, :, part_rows(t)],
            send_sem=e_send.at[e, t],
            recv_sem=e_recv.at[g, t],
            device_id=(y * NX + fifth_x(e), r, y),
            device_id_type=MESH,
        )

    def contract(left, right):
        return lax.dot_general(left, right, (((0,), (0,)), ((), ())), preferred_element_type=f32)

    def chunk_lanes(c):
        return pl.ds(pl.multiple_of((c % NX) * LANE, LANE), LANE)

    def weigh_rows(q, t):
        h = hrow[q * NT + t]
        for s in range(NCH):
            rows = slice(s * LANE, (s + 1) * LANE)
            u = recip(1.0 + h * ldcol[rows, :]).astype(bf16).astype(f32)
            value = rbuf[q, t, rows, :].astype(f32) * u
            lhsy[rows, 0:LANE] = (value * lwcol[rows, :]).astype(bf16)
            lhsy[rows, LANE : 2 * LANE] = value.astype(bf16)

    def pair_sums(q, t):
        weigh_rows(q, t)
        cb = jnp.where(q > y, other, r)
        sums = contract(lhsy[...], colw[cb]).astype(bf16)
        for c in range(NX):
            for i in range(2):
                first = i * LANE + c * PART
                sendy[q * NX + c, i, part_rows(t), :] = sums[first : first + PART]

    def own_sums(t):
        weigh_rows(y, t)
        sums = (
            contract(lhsy[...], colw[other]).astype(bf16),
            contract(lhsy[...], colw[r]).astype(bf16),
        )

        def piece(core, c, k, i):
            d = DIAG[core][c][k]
            rows = slice(i * LANE + c * PART, i * LANE + (c + 1) * PART)
            return sums[d // NX][rows, d % NX * LANE : (d % NX + 1) * LANE]

        def pick(zero, one):
            return jnp.where(r == 0, zero.astype(f32), one.astype(f32)).astype(bf16)

        for i in range(2):
            for c in range(NX):
                for k in range(4):
                    sendy[y * NX + c, i, part_rows(t), k * LANE : (k + 1) * LANE] = pick(
                        piece(0, c, k, i), piece(1, c, k, i)
                    )
            for e in range(2):
                sendx[e, i, part_rows(t), :] = pick(piece(0, 1 + e, 4, i), piece(1, 3 * e, 4, i))

    def deliver(t):
        for dz, dx in ORDER:
            pair_copy((zz + dz) % NQ, (x + dx) % NX, t).start()

        recvy[g, :, part_rows(t), :] = sendy[g, :, part_rows(t), :]

        @pl.loop(0, 2)
        def _(e):
            @pl.when(y * NX + fifth_x(e) == g)
            def _():
                recvx[g, :, part_rows(t), :] = sendx[e, :, part_rows(t), :]

            @pl.when(y * NX + fifth_x(e) != g)
            def _():
                extra_copy(e, t).start()

    def place(j):
        d = (code >> (4 * j)) & 7
        cb = jnp.where(diag, jnp.where(d >= NX, r, other), own_cb)
        return cb, jnp.where(diag, d % NX, j % NX)

    def make_table(rows):
        for k in range(NX + 1):
            cb, chunk = place(k)
            ctab[rows, k * LANE : (k + 1) * LANE] = hcols[cb, rows, chunk_lanes(chunk)]

    make_table(slice(TROWS - 8, TROWS))
    hdr[...] = jnp.zeros((LANE, LANE), f32)
    hdr[R_POS : R_POS + 1, :] = hpos[zz * NX + x]
    hdt[...] = jnp.transpose(hdr[...])

    def weight_sums(b):
        tile = allst[b, T_LD]
        inv = recip(tile)
        h = hdt[:, R_POS : R_POS + 1]
        for c in range(NCH):
            lanes = slice(c * LANE, (c + 1) * LANE)
            row = tile[c : c + 1, :]
            u16 = recip(1.0 + h * row).astype(bf16)
            u = u16.astype(f32)
            lhsw[0:ROWS, lanes] = (u * inv[c : c + 1, :]).astype(bf16)
            lhsw[ROWS : 2 * ROWS, lanes] = u16
            lhsw[2 * ROWS : 3 * ROWS, lanes] = (u * row).astype(bf16)
        ldc = column_tile(tile)
        h = ctab[R_POS : R_POS + 1, 0:TB]
        for c in range(NCH):
            ucol[c * LANE : (c + 1) * LANE, :] = recip(1.0 + ldc[:, c : c + 1] * h).astype(bf16)
        wbuf[b] = jnp.dot(lhsw[...], ucol[...], preferred_element_type=f32)

        @pl.when(fifth)
        def _():
            h = ctab[R_POS : R_POS + 1, TB : TB + LANE]
            for c in range(NCH):
                ucol[c * LANE : (c + 1) * LANE, 0:LANE] = recip(1.0 + ldc[:, c : c + 1] * h).astype(
                    bf16
                )
            wext[b] = jnp.dot(lhsw[...], ucol[:, 0:LANE], preferred_element_type=f32)

    @pl.loop(0, NX)
    def _(step):
        far = (y + 2) % NQ
        for way in range(2):
            part = rbuf.at[far, step, pl.ds(way * (SNP // 2), SNP // 2)]
            pltpu.make_async_copy(part, part, f_recv.at[way, step]).wait()
            part = half_of((y + 3 + 2 * way) % NQ, step, 1 - way)
            pltpu.make_async_copy(part, part, r_recv.at[way, 1, step]).wait()

        @pl.loop(0, NQ)
        def _(k):
            @pl.when(k == y)
            def _():
                own_sums(step)

            @pl.when(k != y)
            def _():
                pair_sums(k, step)

        deliver(step)

        @pl.when(step < NT - 1)
        def _():
            pass_on(step + 1)

        @pl.when(step < NT - 2)
        def _():
            send_chunk(step + 2)

        @pl.loop(0, W_STEP)
        def _(k):
            weight_sums(step * W_STEP + k)


    @pl.loop(NT * W_STEP, NB)
    def _(b):
        weight_sums(b)

    for cb, q in ((r, y), (other, T_OTHER)):
        total = total_of(q)
        for b in range(NB):
            h = scaled(slope(inv_t - inv_b[b], lds_t - lds_b[b], total - allst[b, q], n_del))
            for c in range(NX):
                hcols[cb, b : b + 1, c * LANE : (c + 1) * LANE] = h[c : c + 1, :]
    make_table(slice(0, NB))
    total = total_of(zz)
    h_full = scaled(slope(inv_t, lds_t, total, n_full))
    for c in range(NX):
        hdq[R_FULL, c] = h_full[c : c + 1, :]
    for b in range(NB):
        h = scaled(slope(inv_t - inv_b[b], lds_t - lds_b[b], total - allst[b, zz], n_del))
        for c in range(NX):
            hdq[b, c] = h[c : c + 1, :]
    for b in range(NB + 1):
        hdr[b : b + 1, :] = hdq[b, x]
    hdt[...] = jnp.transpose(hdr[...])

    def factors(weights, parts, full, first, width):
        @pl.loop(0, ROWS // 8)
        def _(t):
            base = pl.multiple_of(t * 8, 8)

            def at(i):
                return pl.ds(i * ROWS + base, 8)

            for c in range(width // LANE):
                lanes = slice(c * LANE, (c + 1) * LANE)
                tlanes = slice(first + c * LANE, first + (c + 1) * LANE)
                tot = [weights[0, at(i), lanes] for i in range(3)]
                for b in range(1, NB):
                    tot = [tot[i] + weights[b, at(i), lanes] for i in range(3)]

                def pair(w, b):
                    scale = hdt[pl.ds(base, 8), b : b + 1] * ctab[b : b + 1, tlanes]
                    k = scale / (w[0] * w[2] - w[1] * w[1])
                    return w[0] * k, w[1] * k

                full[0, pl.ds(base, 8), lanes], full[1, pl.ds(base, 8), lanes] = pair(tot, R_FULL)
                for b in range(NB):
                    w = [tot[i] - weights[b, at(i), lanes] for i in range(3)]
                    parts[b, at(0), lanes], parts[b, at(1), lanes] = pair(w, b)

    factors(wbuf, fbuf, wfull, 0, TB)

    @pl.when(fifth)
    def _():
        factors(wext, fext, wfext, TB, LANE)

    def mirror_copy(j, t):
        cb, chunk = place(j)
        slot = jnp.where(jnp.logical_and(diag, cb == r), NX + x, x)
        return pltpu.make_async_remote_copy(
            src_ref=msend.at[j, :, part_rows(t)],
            dst_ref=mrecv.at[slot, :, part_rows(t)],
            send_sem=m_send.at[j, t],
            recv_sem=m_recv.at[slot, t],
            device_id=(y * NX + chunk, cb, zz),
            device_id_type=MESH,
        )

    def sends(j):
        cb, chunk = place(j)
        return jnp.logical_not(diag & (cb == r) & (chunk == x))

    def finish(pairs, weights, full, j, first, t):
        cb, chunk = place(j)
        out = chunk_lanes(chunk)
        lanes = pl.ds(pl.multiple_of(first, LANE), LANE)

        @pl.loop(0, PART // 16)
        def _(i):
            base = pl.multiple_of(t * PART + i * 16, 16)
            rows = pl.ds(base, 16)
            tot0 = pairs[0, 0, rows, lanes].astype(f32)
            tot1 = pairs[0, 1, rows, lanes].astype(f32)
            for b in range(1, NB):
                tot0 = tot0 + pairs[b, 0, rows, lanes].astype(f32)
                tot1 = tot1 + pairs[b, 1, rows, lanes].astype(f32)
            rg = full[0, rows, lanes] * tot1 - full[1, rows, lanes] * tot0
            rg_ref[cb, rows, out] = rg
            msend[j, 0, rows, :] = rg.astype(bf16)
            values = []
            for b in range(NB):
                del0 = tot0 - pairs[b, 0, rows, lanes].astype(f32)
                del1 = tot1 - pairs[b, 1, rows, lanes].astype(f32)
                values.append(
                    weights[b, pl.ds(base, 16), lanes] * del1
                    - weights[b, pl.ds(ROWS + base, 16), lanes] * del0
                )
            mean = functools.reduce(jnp.add, values) * (1.0 / NB)
            spread = functools.reduce(jnp.add, [(v - mean) * (v - mean) for v in values])
            se = jnp.sqrt((NB - 1) / NB * spread)
            se_ref[cb, rows, out] = se
            msend[j, 1, rows, :] = se.astype(bf16)

        @pl.when(sends(j))
        def _():
            mirror_copy(j, t).start()

    @pl.loop(0, NT)
    def _(t):
        @pl.loop(1, NB)
        def _(k):
            part = recvy.at[(g + k) % NB, :, part_rows(t)]
            pltpu.make_async_copy(part, part, a_recv.at[(g + k) % NB, t]).wait()

        @pl.loop(0, NX)
        def _(j):
            finish(recvy, fbuf, wfull, j, j * LANE, t)

        @pl.when(fifth)
        def _():
            @pl.loop(1, NB)
            def _(k):
                part = recvx.at[(g + k) % NB, :, part_rows(t)]
                pltpu.make_async_copy(part, part, e_recv.at[(g + k) % NB, t]).wait()

            finish(recvx, fext, wfext, NX, 0, t)

    def take(slot, cb, chunk):
        @pl.loop(0, NT)
        def _(t):
            part = mrecv.at[slot, :, part_rows(t)]
            pltpu.make_async_copy(part, part, m_recv.at[slot, t]).wait()

        lanes = chunk_lanes(chunk)
        rg_ref[cb, :, lanes] = jnp.transpose(mrecv[slot, 0].astype(f32))
        se_ref[cb, :, lanes] = jnp.transpose(mrecv[slot, 1].astype(f32))

    @pl.when(jnp.logical_not(diag))
    def _():
        @pl.loop(0, NX)
        def _(k):
            take(k, 1 - own_cb, k)

    @pl.when(diag)
    def _():
        chunks = 4 + jnp.where(fifth, 1, 0)

        @pl.loop(0, 2 * NX)
        def _(d):
            taken = jnp.int32(0)
            for k in range(NX + 1):
                hit = ((code >> (4 * k)) & 7) == d
                taken = taken + jnp.where(jnp.logical_and(hit, k < chunks), 1, 0)

            @pl.when(taken == 0)
            def _():
                take(d, jnp.where(d >= NX, r, other), d % NX)

    @pl.loop(1, NQ)
    def _(k):
        y_copy(k).wait_send()

    core_copy(stage.at[y], stage.at[T_OTHER], 0).wait_send()
    core_copy(z_ref, cbuf, 1).wait_send()

    @pl.loop(0, NX)
    def _(c):
        for way in range(2):
            row_copy(way, c, 0).wait_send()
            row_copy(way, c, 1).wait_send()
            far_copy(way, c).wait_send()

    @pl.loop(1, NB)
    def _(k):
        g_copy(k).wait_send()
        p = (g + k) % NB

        @pl.loop(0, NT)
        def _(t):
            pair_copy(p // NX, p % NX, t).wait_send()

    @pl.loop(0, NT)
    def _(t):
        @pl.loop(0, 2)
        def _(e):
            @pl.when(y * NX + fifth_x(e) != g)
            def _():
                extra_copy(e, t).wait_send()

        @pl.loop(0, NX)
        def _(j):
            @pl.when(sends(j))
            def _():
                mirror_copy(j, t).wait_send()

        @pl.when(fifth)
        def _():
            mirror_copy(NX, t).wait_send()


def per_device(ldscore, zscores):
    dma = pltpu.SemaphoreType.DMA
    out = jax.ShapeDtypeStruct((2, ROWS, TB), f32)
    rg, se = pl.pallas_call(
        kernel,
        out_shape=(out, out),
        in_specs=[pl.BlockSpec(memory_space=pltpu.VMEM)] * 2,
        out_specs=[pl.BlockSpec(memory_space=pltpu.VMEM)] * 2,
        scratch_shapes=[
            pltpu.VMEM((T_LD + 1, 8, LANE), f32),
            pltpu.VMEM((NB, T_LD + 1, 8, LANE), f32),
            pltpu.VMEM((SNP, LANE), f32),
            pltpu.VMEM((SNP, LANE), f32),
            pltpu.VMEM((NQ * NT, 1, LANE), f32),
            pltpu.VMEM((NQ * NX, 1, LANE), f32),
            pltpu.VMEM((R_POS + 1, NX, 1, LANE), f32),
            pltpu.VMEM((LANE, LANE), f32),
            pltpu.VMEM((LANE, LANE), f32),
            pltpu.VMEM((2, TROWS, TB), f32),
            pltpu.VMEM((TROWS, TB + LANE), f32),
            pltpu.VMEM((NQ, NT, SNP, LANE), bf16),
            pltpu.VMEM((SNP, TB), bf16),
            pltpu.VMEM((2, SNP, TB), bf16),
            pltpu.VMEM((SNP, 2 * LANE), bf16),
            pltpu.VMEM((NB, 2, ROWS, TB), bf16),
            pltpu.VMEM((2, 2, ROWS, LANE), bf16),
            pltpu.VMEM((NB, 2, ROWS, TB), bf16),
            pltpu.VMEM((NB, 2, ROWS, LANE), bf16),
            pltpu.VMEM((3 * ROWS, SNP), bf16),
            pltpu.VMEM((SNP, TB), bf16),
            pltpu.VMEM((NB, 3 * ROWS, TB), f32),
            pltpu.VMEM((NB, 3 * ROWS, LANE), f32),
            pltpu.VMEM((NB, 2 * ROWS, TB), f32),
            pltpu.VMEM((NB, 2 * ROWS, LANE), f32),
            pltpu.VMEM((2, ROWS, TB), f32),
            pltpu.VMEM((2, ROWS, LANE), f32),
            pltpu.VMEM((NX + 1, 2, LANE, LANE), bf16),
            pltpu.VMEM((2 * NX, 2, LANE, LANE), bf16),
            dma((NQ,)),
            dma((NQ,)),
            dma((NB,)),
            dma((NB,)),
            dma((2,)),
            dma((2,)),
            dma((2, 2, NT)),
            dma((2, 2, NT)),
            dma((2, NT)),
            dma((2, NT)),
            dma((NB, NT)),
            dma((NB, NT)),
            dma((2, NT)),
            dma((NB, NT)),
            dma((NX + 1, NT)),
            dma((2 * NX, NT)),
        ],
        compiler_params=pltpu.CompilerParams(
            collective_id=0, has_side_effects=True, vmem_limit_bytes=56 * 1024 * 1024
        ),
    )(ldscore.reshape(8, LANE), zscores)
    return (rg.transpose(1, 0, 2)[None], se.transpose(1, 0, 2)[None])


def solution(mesh):
    return jax.shard_map(
        per_device,
        mesh=mesh,
        in_specs=(P("genome"), P("genome", ("trow", "tcol"))),
        out_specs=(P("trow", "genome", None, "tcol"), P("trow", "genome", None, "tcol")),
        check_vma=False,
    )
```
